256 devices in a mesh: dp: 32 (over y_hi, z, core), blk: 8 (over x, y_lo).
Axes of the slice: x: 4, y: 4 (y_hi: 2, y_lo: 2; y = y_hi * 2 + y_lo), z: 8, core: 2. Of those that a mesh axis runs over, the one named last changes fastest.
Arguments:
- patches: bfloat16 [32, 8, 256, 1152], P('dp', 'blk'), may hold values from -8 to 8
- counts: int32 [32, 8, 1], P('dp', 'blk'), may hold values from 1 to 256, as said below
- norm_gain: float32 [1152], replicated, may hold values from 0.1 to 1.9
- norm_bias: float32 [1152], replicated, may hold values from -3 to 3
- weight_in: bfloat16 [1152, 4304], P('dp'), may hold values from -0.1875 to 0.1875
- bias_in: float32 [4304], replicated, may hold values from -3 to 3
- weight_out: bfloat16 [4304, 1152], P(None, 'dp'), may hold values from -0.09375 to 0.09375
- bias_out: float32 [1152], replicated, may hold values from -3 to 3
- text_embed: bfloat16 [256, 1152], P(('dp', 'blk')), may hold values from -0.19921875 to 0.19921875
- pair_label: int32 [256], replicated, may hold values from 0 to 63
- logit_params: float32 [2], replicated, may hold values from -5 to 2.5, as said below
Outputs:
- patch_grad: bfloat16 [32, 8, 256, 1152], P('dp', 'blk')
- text_grad: bfloat16 [256, 1152], P(('dp', 'blk'))
- statistics: float32 [3], replicated
The draws below stay inside these ranges and needn't reach their ends.
Inputs may be any that keep to these rules, and one draw needn't show every extreme that they name: `counts`: the count of each device is 8 times a whole number from 1 to 32; over the devices of one blk index they sum to 4096; on one device of each blk index every count is 256. `logit_params`: the first entry is the logarithm of the logit scale, the second the logit bias.
All inputs are finite; a program needn't handle non-finite values.
Results may differ from the reference program's by a relative error of at most 0.0056.
Values may be sent and summed in bfloat16 or wider, within the bound.
A program may use at most 128 MiB of HBM per device.

```python
import math
import jax
import jax.numpy as jnp
import numpy as np
from jax import lax

D = 1152
FF = 4304
MAXP = 256
ROWS_DEV = 128
IMG_DEV = 1
CAP = 8
PAIRS = 256
LABELS = 64
N_DP = 32
N_BLK = 8


def draw_patches(key, part):
    key = jax.random.fold_in(key, 5)
    offset_key, row_key = jax.random.split(key)
    offsets = jax.random.normal(offset_key, (N_DP, N_BLK, IMG_DEV, 1, D), jnp.float32)
    rows = jax.random.normal(row_key, (N_DP, N_BLK, IMG_DEV, MAXP, D), jnp.float32)
    values = jnp.clip(rows + offsets, -8.0, 8.0)
    return values.reshape(N_DP, N_BLK, IMG_DEV * MAXP, D).astype(jnp.bfloat16)


def draw_counts(key, part):
    key = jax.random.fold_in(key, 11)
    slot_cap = CAP
    image_total = IMG_DEV
    dp_count = N_DP

    def column(column_key):
        perm_key, degree_key, adjust_key = jax.random.split(column_key, 3)
        half_count = dp_count // 2
        first_half = jax.random.randint(degree_key, (half_count,), 1, dp_count)
        first_half = first_half.at[0].set(dp_count).at[1].set(1)
        second_half = dp_count - first_half
        second_half = second_half.at[0].set(1).at[1].set(dp_count - 2)
        values = jnp.concatenate([first_half, second_half]).astype(jnp.int32)
        device_order = jax.random.permutation(perm_key, dp_count)
        degrees = jnp.zeros((dp_count,), jnp.int32).at[device_order].set(values)
        row_totals = degrees * slot_cap
        base_count = row_totals // image_total
        extra_rows = row_totals - base_count * image_total
        slot_ids = jnp.arange(image_total, dtype=jnp.int32)
        start_counts = base_count[:, None] + (slot_ids[None, :] < extra_rows[:, None]).astype(jnp.int32)
        partner = slot_ids + 1 - 2 * (slot_ids % 2)
        has_pair = partner < image_total
        partner_safe = jnp.minimum(partner, image_total - 1)
        partner_counts = start_counts[:, partner_safe]
        lowest = jnp.minimum(start_counts, partner_counts)
        highest = jnp.maximum(start_counts, partner_counts)
        room_left = jnp.maximum(jnp.minimum(lowest - 1, MAXP - highest), 0)
        raw_bits = jax.random.randint(adjust_key, (dp_count, image_total), 0, 1 << 20)
        even_room = room_left[:, slot_ids - slot_ids % 2]
        even_bits = raw_bits[:, slot_ids - slot_ids % 2]
        shift_amount = even_bits % (even_room + 1)
        adjust_by = jnp.where(has_pair[None, :], jnp.where((slot_ids % 2)[None, :] == 0, shift_amount, -shift_amount), 0)
        return (start_counts + adjust_by).astype(jnp.int32)
    column_keys = jax.vmap(lambda index: jax.random.fold_in(key, index))(jnp.arange(N_BLK))
    columns = jax.vmap(column)(column_keys)
    return jnp.transpose(columns, (1, 0, 2)).astype(jnp.int32)


def draw_logit_params(key, part):
    key = jax.random.fold_in(key, 23)
    scale_key, bias_key = jax.random.split(key)
    log_scale = jax.random.uniform(scale_key, (), jnp.float32, 1.5, 2.5)
    logit_bias = jax.random.uniform(bias_key, (), jnp.float32, -5.0, -2.0)
    return jnp.stack([log_scale, logit_bias]).astype(jnp.float32)


def with_ends(entries, own_key, smallest, top_value):
    extent = entries.shape
    spot = [jax.random.randint(jax.random.fold_in(own_key, axis), (), 0, extent[axis]) for axis in range(len(extent))]
    entries = entries.at[tuple(spot)].set(smallest)
    longest = extent.index(max(extent))
    spot[longest] = (spot[longest] + 1) % extent[longest]
    return entries.at[tuple(spot)].set(top_value)


def level_of(rng, shape, cuts, low, high):
    loudness = 1.0
    for position, parts in cuts:
        heights = jax.random.uniform(jax.random.fold_in(jax.random.fold_in(rng, 6), position), (parts,), jnp.float32, low / len(cuts), high / len(cuts))
        loudness = loudness * jnp.repeat(jnp.exp(heights), shape[position] // parts).reshape((-1,) + (1,) * (len(shape) - 1 - position))
    return loudness


def cumulative_ranks(count, lean):
    weights = [(1 << 20) // math.isqrt(grade ** lean) + 1 for grade in range(1, count + 1)]
    deviation = 1 + sum(weights) // (1 << 30)
    return np.cumsum(np.array([max(1, weight // deviation) for weight in weights]))


def ranked_ids(rng, dims, number_of, skew):
    grid = cumulative_ranks(number_of, skew)
    ticket = jax.random.randint(jax.random.fold_in(rng, 1), dims, 0, int(grid[number_of - 1]))
    standing = jnp.searchsorted(jnp.asarray(grid, jnp.int32), ticket, side="right")
    return jax.random.permutation(jax.random.fold_in(rng, 2), number_of)[standing].astype(jnp.int32)


def scatter_about(rng, shape, spread, limit, shards=(), held_as=jnp.bfloat16):
    entries = jax.random.normal(rng, shape, jnp.float32) * spread
    if len(shards) > 0:
        entries = level_of(rng, shape, shards, -0.22, 0.18) * entries
    return jnp.clip(entries, min=-limit, max=limit).astype(held_as)


def setup_inputs(seed: int = 0) -> dict:
    key_list = jax.random.split(jax.random.key(seed), 12)
    return {
        "patches": draw_patches(jax.random.fold_in(key_list[11], 71), 0),
        "counts": draw_counts(jax.random.fold_in(key_list[11], 71), 0),
        "norm_gain": jnp.clip(1.0 + 0.18 * jax.random.normal(key_list[2], (D,), jnp.float32), 0.1, 1.9),
        "norm_bias": scatter_about(key_list[3], (D,), 0.5, 3.0, (), jnp.float32),
        "weight_in": scatter_about(key_list[4], (D, FF), D ** -0.5, 0.1875, ((0, 32),)),
        "bias_in": scatter_about(key_list[5], (FF,), 0.5, 3.0, (), jnp.float32),
        "weight_out": scatter_about(key_list[6], (FF, D), FF ** -0.5, 0.09375, ((1, 32),)),
        "bias_out": scatter_about(key_list[7], (D,), 0.5, 3.0, (), jnp.float32),
        "text_embed": scatter_about(key_list[8], (PAIRS, D), 0.03, 0.19921875, ((0, 256),)),
        "pair_label": with_ends(ranked_ids(key_list[9], (PAIRS,), LABELS, 2), jax.random.fold_in(key_list[9], 3), 0, LABELS - 1).astype(jnp.int32),
        "logit_params": draw_logit_params(jax.random.fold_in(key_list[11], 71), 0),
    }


NORM_EPS = 1e-06
GELU_SCALE = 0.7978845608028654
GELU_CUBIC = 0.044715

def gelu_parts(pre_act):
    inner = GELU_SCALE * (pre_act + GELU_CUBIC * pre_act * pre_act * pre_act)
    tanh_vals = jnp.tanh(inner)
    value = 0.5 * pre_act * (1.0 + tanh_vals)
    slope = 0.5 * (1.0 + tanh_vals) + 0.5 * pre_act * (1.0 - tanh_vals * tanh_vals) * GELU_SCALE * (1.0 + 3.0 * GELU_CUBIC * pre_act * pre_act)
    return (value, slope)

def layer_norm(rows, norm_gain, norm_bias):
    wide_rows = rows.astype(jnp.float32)
    centre = wide_rows - lax.optimization_barrier(jnp.mean(wide_rows, axis=-1, keepdims=True))
    inv_std = lax.rsqrt(lax.optimization_barrier(jnp.mean(centre * centre, axis=-1, keepdims=True)) + NORM_EPS)
    plain_rows = centre * inv_std
    return (plain_rows, inv_std, (plain_rows * norm_gain + norm_bias).astype(jnp.bfloat16))

def contract_last(left, right):
    return lax.dot_general(left, right, (((1,), (1,)), ((), ())), preferred_element_type=jnp.float32)

def reference(patches, counts, norm_gain, norm_bias, weight_in, bias_in, weight_out, bias_out, text_embed, pair_label, logit_params):
    flat_counts = counts.reshape(-1).astype(jnp.int32)
    image_ends = jnp.cumsum(flat_counts).astype(jnp.int32)
    image_starts = image_ends - flat_counts
    total_rows = N_DP * N_BLK * ROWS_DEV
    row_ids = jnp.arange(total_rows, dtype=jnp.int32)
    image_of = jnp.searchsorted(image_ends, row_ids, side='right').astype(jnp.int32)
    source_rows = (image_of * MAXP + row_ids - image_starts[image_of]).astype(jnp.int32)
    flat_rows = patches.reshape(PAIRS * MAXP, D)
    work_rows = jnp.take(flat_rows, source_rows, axis=0).reshape(-1, ROWS_DEV, D)

    def forward_block(block_rows):
        plain_rows, inv_std, normed = layer_norm(block_rows, norm_gain, norm_bias)
        pre_act = jnp.dot(normed, weight_in, preferred_element_type=jnp.float32) + bias_in
        hidden, gelu_slope = gelu_parts(pre_act)
        mixed = jnp.dot(hidden.astype(jnp.bfloat16), weight_out, preferred_element_type=jnp.float32)
        return block_rows.astype(jnp.float32) + mixed + bias_out
    out_rows = lax.map(forward_block, work_rows).reshape(total_rows, D)
    count_f = flat_counts.astype(jnp.float32)
    pooled = jax.ops.segment_sum(out_rows, image_of, num_segments=PAIRS) / count_f[:, None]
    img_norm = jnp.sqrt(lax.optimization_barrier(jnp.sum(pooled * pooled, axis=1, keepdims=True)) + NORM_EPS)
    img_unit = pooled / img_norm
    img_b = img_unit.astype(jnp.bfloat16)
    text_f = text_embed.astype(jnp.float32)
    txt_norm = jnp.sqrt(lax.optimization_barrier(jnp.sum(text_f * text_f, axis=1, keepdims=True)) + NORM_EPS)
    txt_unit = text_f / txt_norm
    txt_b = txt_unit.astype(jnp.bfloat16)
    logit_scale = jnp.exp(logit_params[0])
    logit_bias = logit_params[1]
    inner_prod = contract_last(img_b, txt_b)
    logit_vals = logit_scale * inner_prod + logit_bias
    sign_vals = jnp.where(pair_label[:, None] == pair_label[None, :], 1.0, -1.0).astype(jnp.float32)
    margins = sign_vals * logit_vals
    logit_grad = -sign_vals * jax.nn.sigmoid(-margins)
    statistics = jnp.stack([jnp.sum(jax.nn.softplus(-margins)), jnp.sum(logit_grad * logit_scale * inner_prod), jnp.sum(logit_grad)]) / PAIRS
    d_img = logit_scale * jnp.dot(logit_grad, txt_b.astype(jnp.float32), precision=lax.Precision.HIGHEST)
    d_txt = logit_scale * jnp.dot(logit_grad.T, img_b.astype(jnp.float32), precision=lax.Precision.HIGHEST)
    text_grad = ((d_txt - txt_unit * lax.optimization_barrier(jnp.sum(txt_unit * d_txt, axis=1, keepdims=True))) / txt_norm).astype(jnp.bfloat16)
    d_pooled = (d_img - img_unit * lax.optimization_barrier(jnp.sum(img_unit * d_img, axis=1, keepdims=True))) / img_norm
    row_grad = jnp.take(d_pooled / count_f[:, None], image_of, axis=0).reshape(-1, ROWS_DEV, D)

    def backward_block(pair_rows):
        block_rows, block_grad = pair_rows
        plain_rows, inv_std, normed = layer_norm(block_rows, norm_gain, norm_bias)
        pre_act = jnp.dot(normed, weight_in, preferred_element_type=jnp.float32) + bias_in
        hidden, gelu_slope = gelu_parts(pre_act)
        act_grad = contract_last(block_grad.astype(jnp.bfloat16), weight_out)
        pre_grad = (act_grad * gelu_slope).astype(jnp.bfloat16)
        normed_grad = contract_last(pre_grad, weight_in)
        plain_grad = normed_grad * norm_gain
        input_grad = inv_std * (plain_grad - lax.optimization_barrier(jnp.mean(plain_grad, axis=-1, keepdims=True)) - plain_rows * lax.optimization_barrier(jnp.mean(plain_grad * plain_rows, axis=-1, keepdims=True)))
        return (MAXP * (block_grad + input_grad)).astype(jnp.bfloat16)
    row_results = lax.map(backward_block, (work_rows, row_grad)).reshape(total_rows, D)
    patch_grad = jnp.zeros((PAIRS * MAXP, D), jnp.bfloat16).at[source_rows].set(row_results).reshape(patches.shape)
    return (patch_grad, text_grad, statistics)
```

```python
import jax
import jax.numpy as jnp
from jax import lax
from jax.experimental import pallas as pl
from jax.experimental.pallas import tpu as pltpu
from jax.sharding import PartitionSpec as P

D = 1152
FF = 4304
ROWS = 256
NORM_EPS = 1e-06
GELU_SCALE = 0.7978845608028654
GELU_CUBIC = 0.044715
MESH = pl.DeviceIdType.MESH
F32 = jnp.float32
BF16 = jnp.bfloat16
NT_IN = 34
N_COPIES = 180


def dev(x, y, z, c):
    x, y, z, c = x % 4, y % 4, z % 8, c % 2
    return ((y // 2) * 16 + z * 2 + c, x * 2 + y % 2)


def nt_dot(a, b):
    return lax.dot_general(a, b, (((1,), (1,)), ((), ())), preferred_element_type=F32)


def nn_dot(a, b):
    return jnp.dot(a, b, preferred_element_type=F32)


def split3(v):
    hi = v.astype(BF16)
    rest = v - hi.astype(F32)
    mid = rest.astype(BF16)
    low = (rest - mid.astype(F32)).astype(BF16)
    return hi, mid, low


def exact_dot(v, w, dot):
    rows = v.shape[0]
    hi, mid, low = split3(v)
    res = dot(jnp.concatenate([hi, mid, low], axis=0), w)
    return res[:rows] + res[rows : 2 * rows] + res[2 * rows :]


def rows8(v):
    return jnp.broadcast_to(v, (8, v.shape[1]))


def kernel(
    x_ref, wi_ref, wo_ref, vec_ref, bin_ref, labl_ref, lab2_ref, sc_ref,
    out_ref, tg_ref, st_ref,
    G, W, PM, XP, PLAIN, RSTD, NM, SL, HS, AF, ACC, RW, RO, SF, VP,
    TROW, TCOL, TB, HA, PB, PR, GB, AB, AR, ICOL, DB, DT,
    SS, RS,
):
    dp, blk = lax.axis_index("dp"), lax.axis_index("blk")
    yh, z, c = dp // 16, (dp // 2) % 8, dp % 2
    x, yl = blk // 2, blk % 2
    y = yh * 2 + yl
    cross = dev(x, y + 3 + 2 * yl, z, c)
    share = dev(x, yh * 2 + 1 - yl, z, c)
    partner = dev(x, y, z, c + 1)
    zp, zm = dev(x, y, z + 1, c), dev(x, y, z + 7, c)
    xp, xm = dev(x + 1, y, z, c), dev(x + 3, y, z, c)
    u, v, s = z * 2 + c, x * 4 + y, x * 2 + c
    col_peers = [((u + d) % 16) for d in range(1, 16)]
    col_devs = [dev(x, y, p // 2, p % 2) for p in col_peers]
    plane_peers = [((v + d) % 16) for d in range(1, 16)]
    plane_devs = [dev(p // 4, p % 4, z, c) for p in plane_peers]
    ring_peers = [((s + d) % 8) for d in range(1, 8)]
    ring_devs = [dev(p // 2, y, z, p % 2) for p in ring_peers]

    bar = pltpu.get_barrier_semaphore()
    greet = col_devs + plane_devs + [dev(x + d, y, z, c + 1) for d in (1, 2, 3)]
    for peer in greet:
        pl.semaphore_signal(bar, inc=1, device_id=peer, device_id_type=MESH)

    copies = {}

    def send(name, src, dst, device):
        k = len(copies)
        cp = pltpu.make_async_remote_copy(
            src_ref=src, dst_ref=dst, send_sem=SS.at[k], recv_sem=RS.at[k], device_id=device, device_id_type=MESH
        )
        cp.start()
        copies[name] = cp

    def same(name, ref, device):
        send(name, ref, ref, device)

    def got(name):
        copies[name].wait_recv()

    def fold(rows, first, count):
        parts = []
        for a in range(0, 8, 2):
            blocks = []
            for b in range(2):
                if a + b < count:
                    t = first + a + b
                    piece = rows[:, 128 * t : 128 * t + 128]
                    blocks.append(pltpu.roll(piece, 4, 0) if b else piece)
            parts.append(sum(blocks) if blocks else jnp.zeros((8, 128), F32))
        return jnp.concatenate(parts, axis=0).astype(BF16)

    wi_tail = wi_ref[32:48, :].astype(F32)[0:8]
    for q in range(4):
        for t in range(8):
            G[yh, z, c, q, 5 * (t // 4) + t % 4] = wi_ref[0:32, 1024 * q + 128 * t : 1024 * q + 128 * t + 128]
        G[yh, z, c, q, 4] = fold(wi_tail, 8 * q, 8)
    eye = (
        lax.broadcasted_iota(jnp.int32, (48, 36), 0) == lax.broadcasted_iota(jnp.int32, (48, 36), 1)
    ).astype(F32).astype(BF16)
    wo_first = 8 * x + x // 2
    wo_rows = wo_ref[pl.ds(pl.multiple_of(128 * wo_first, 128), 1152), :]
    wo_t = nt_dot(eye, wo_rows)
    wo_main = wo_t[0:32].astype(BF16)
    for t in range(2):
        W[yh, z, c, t] = wi_ref[0:32, 4096 + 128 * t : 4096 + 128 * t + 128]
    for t in range(9):
        W[yh, z, c, 2 + t] = wo_main[:, 128 * t : 128 * t + 128]
    tail = jnp.concatenate([wi_tail[:, 4096:4352], wo_t[32:40]], axis=1)
    W[yh, z, c, 11] = fold(tail, 0, 8)
    W[yh, z, c, 12] = fold(tail, 8, 3)

    pl.semaphore_wait(bar, len(greet))

    def zz(d):
        return (z + 8 + d) % 8

    other = 1 - yh
    both = slice(None)
    mine5 = pl.ds(4 * yl, 5)
    mine4 = pl.ds(5 * yl, 4)
    pair0 = 2 * (x // 2)
    pair1 = 2 - pair0

    def z_in(n):
        if n < 4:
            got(("zR", n - 1))
            got(("zL", n - 1))
            if n == 1:
                got(("zRb", 0))
                got(("zLb", 0))
            sel_r = both if n < 3 else 0
            sel_l = both if n < 3 else 1
            same(("zR", n), G.at[sel_r, zz(-n), c, x, mine5], zp)
            same(("zL", n), G.at[sel_l, zz(n), c, x, mine5], zm)
        else:
            got(("zR", 3))
            got(("zL", 3))

    def d_in(n):
        if n == 0:
            got(("d1",))
        else:
            got(("dR", n - 1))
            got(("dL", n - 1))
        if n < 4:
            sel_r = both if n < 3 else 0
            sel_l = both if n < 3 else 1
            same(("dR", n), W.at[sel_r, zz(-n), c], zp)
            same(("dL", n), W.at[sel_l, zz(n), c], zm)

    def d_partner(dz):
        same(("pD", dz), W.at[:, zz(dz), c], partner)

    def x_send(dz):
        sel = other if dz == 0 else both
        same(("xR", dz), G.at[sel, zz(dz), c, x, mine5], xp)
        same(("xL", dz), G.at[sel, zz(dz), c, x, mine5], xm)

    def x_in(dz):
        got(("xR", dz))
        got(("xL", dz))
        same(("fR", dz), G.at[other if dz == 0 else 0, zz(dz), c, (x + 3) % 4, mine5], xp)
        if dz != 0:
            same(("fL", dz), G.at[1, zz(dz), c, (x + 1) % 4, mine5], xm)
            same(("yC", dz), G.at[:, zz(dz), c, pl.ds(pair0, 2), mine4], cross)

    def f_in(dz):
        got(("fR", dz))
        if dz != 0:
            got(("fL", dz))
        sel = other if dz == 0 else both
        same(("yS", dz), G.at[sel, zz(dz), c, pl.ds(pair1, 2), mine4], share)

    def y_in(dz):
        got(("yC", dz))
        got(("yS", dz))
        same(("pG", dz), G.at[:, zz(dz), c], partner)

    same(("e1",), G.at[yh, z, c, x, pl.ds(4 * (1 - yl), 5)], cross)
    same(("zR", 0), G.at[yh, z, c, x, mine5], zp)
    same(("zL", 0), G.at[yh, z, c, x, mine5], zm)
    same(("yC", 0), G.at[yh, z, c, pl.ds(pair0, 2), mine4], cross)
    same(("d1",), W.at[yh, z, c], cross)

    lane = lax.broadcasted_iota(jnp.int32, (1, D), 1)
    rest = lane - 1024
    natural = jnp.where(lane < 1024, 36 * (lane >> 5) + (lane & 31), 36 * (rest >> 2) + 32 + (rest & 3))

    @pl.loop(0, 9)
    def _(i):
        first = pl.multiple_of(128 * i, 128)
        rows = lax.broadcasted_iota(jnp.int32, (128, D), 0) + 128 * i
        PM[pl.ds(first, 128), :] = jnp.where(rows == natural, 1.0, 0.0).astype(BF16)

    got(("e1",))
    same(("zRb", 0), G.at[other, z, c, x, mine5], zp)
    same(("zLb", 0), G.at[other, z, c, x, mine5], zm)
    x_send(0)

    VP[...] = exact_dot(vec_ref[...], PM[...], nn_dot)
    gain, nbias, bout, text_f = VP[0:1, :], VP[1:2, :], VP[2:3, :], VP[3:4, :]
    txt_norm = jnp.sqrt(jnp.sum(text_f * text_f, axis=1, keepdims=True) + NORM_EPS)
    txt_unit = text_f / txt_norm
    TROW[...] = txt_unit
    TCOL[u] = jnp.concatenate([txt_unit.astype(BF16).astype(F32), jnp.zeros((1, 128), F32)], axis=1)
    for i, device in enumerate(col_devs):
        same(("t1", i), TCOL.at[u], device)

    z_in(1)
    x_send(-1)
    x_send(1)
    x_in(0)

    count = sc_ref[2:3, 0:1]

    @pl.loop(0, 4)
    def _(i):
        rows = pl.ds(pl.multiple_of(64 * i, 64), 64)
        xs = nn_dot(x_ref[rows, :], PM[...])
        XP[rows, :] = xs
        centre = xs - jnp.mean(xs, axis=1, keepdims=True)
        inv = lax.rsqrt(jnp.mean(centre * centre, axis=1, keepdims=True) + NORM_EPS)
        plain = centre * inv
        PLAIN[rows, :] = plain
        RSTD[rows, :] = jnp.broadcast_to(inv, (64, 128))
        NM[rows, :] = (plain * gain + nbias).astype(BF16)

    f_in(0)
    for i in range(15):
        got(("t1", i))
    block = TCOL[...].reshape(16, 1280).astype(BF16)
    TB[c, v] = jnp.where(c == 0, block[:, :640].astype(F32), block[:, 640:].astype(F32)).astype(BF16)
    for i, device in enumerate(plane_devs):
        same(("t2", i), TB.at[c, v], device)

    z_in(2)
    x_send(-2)
    x_send(2)
    x_in(-1)
    x_in(1)
    y_in(0)
    z_in(3)
    x_send(-3)
    x_send(3)
    x_in(-2)
    x_in(2)
    f_in(-1)
    f_in(1)
    z_in(4)
    x_send(4)
    d_in(0)
    y_in(-1)
    y_in(1)
    d_partner(0)
    x_in(-3)
    x_in(3)
    f_in(-2)
    f_in(2)
    y_in(-2)
    y_in(2)
    for i in range(15):
        got(("t2", i))
    same(("t3",), TB.at[c], partner)

    row_ids = lax.broadcasted_iota(jnp.int32, (ROWS, 1), 0).astype(F32)
    valid = row_ids < count
    xsum = jnp.sum(jnp.where(valid, XP[...], 0.0), axis=0, keepdims=True)

    @pl.loop(0, 8)
    def _(i):
        r = lax.broadcasted_iota(jnp.int32, (128, 1024), 0)
        col = lax.broadcasted_iota(jnp.int32, (128, 1024), 1)
        SF[pl.ds(pl.multiple_of(128 * i, 128), 128), :] = jnp.where(
            col == 32 * (r >> 2) + 4 * i + (r & 3), 1.0, 0.0
        ).astype(BF16)

    x_in(4)
    f_in(-3)
    f_in(3)
    d_in(1)
    d_partner(-1)
    d_partner(1)
    y_in(-3)
    y_in(3)
    f_in(4)
    d_in(2)
    d_partner(-2)
    d_partner(2)
    y_in(4)
    d_in(3)
    d_partner(-3)
    d_partner(3)
    d_in(4)
    d_partner(4)
    order = (0, -1, 1, -2, 2, -3, 3, 4)
    for dz in order:
        got(("pG", dz))
    for dz in order:
        got(("pD", dz))
    got(("t3",))

    def unfold(store, pieces):
        res = nn_dot(SF[...], jnp.concatenate([p.reshape(1024, 128) for p in pieces], axis=1)).astype(BF16)
        for j in range(len(pieces)):
            for a in range(8):
                store(j, a, res[128 * a : 128 * a + 128, 128 * j : 128 * j + 128])

    def store_in(base):
        def store(j, a, tile):
            RW[8 * (base + j) + a] = tile
        return store

    def store_direct(j, a, tile):
        t = 8 * j + a
        if t < 2:
            RW[32 + t] = tile
        elif t < 11:
            RO[t - 2] = tile

    for q in (0, 2):
        unfold(store_in(q), [G[:, :, :, q, 4], G[:, :, :, q + 1, 4]])
    unfold(store_direct, [W[:, :, :, 11], W[:, :, :, 12]])

    def fwd(first, count_tiles, main_tiles):
        wm = jnp.concatenate([m.reshape(1024, 128) for m in main_tiles], axis=1)
        wr = jnp.concatenate([RW[first + t] for t in range(count_tiles)], axis=1)
        pre_all = nn_dot(NM[:, :1024], wm) + nn_dot(NM[:, 1024:], wr)
        for t in range(count_tiles):
            pre = pre_all[:, 128 * t : 128 * t + 128] + bin_ref[first + t]
            sq = pre * pre
            th = jnp.tanh(GELU_SCALE * pre * (1.0 + GELU_CUBIC * sq))
            half = 0.5 * (1.0 + th)
            hid = pre * half
            SL[first + t] = half + 0.5 * pre * (1.0 - th * th) * (GELU_SCALE + 3.0 * GELU_SCALE * GELU_CUBIC * sq)
            HS[first + t] = jnp.sum(jnp.where(valid, hid, 0.0), axis=0, keepdims=True)

    @pl.loop(0, 8)
    def _(p):
        q, half = p // 2, p % 2
        fwd(4 * p, 4, [G[:, :, :, q, 5 * half + t] for t in range(4)])

    fwd(32, 2, [W[:, :, :, 0], W[:, :, :, 1]])

    def first_tile(member):
        return 4 * member + member // 4

    for i, (p, device) in enumerate(zip(ring_peers, ring_devs)):
        send(("h", i), HS.at[pl.ds(first_tile(p), 5)], HA.at[s], device)
    HA[s] = HS[pl.ds(first_tile(s), 5)]
    for i in range(7):
        got(("h", i))
    last_mine = jnp.where(s % 4 == 3, 1.0, 0.0)
    part_m = jnp.zeros((24, 1024), F32)
    part_r = jnp.zeros((24, 128), F32)
    for t in range(5):
        col = HA[:, t].reshape(8, 128)
        if t == 4:
            col = col * last_mine
        lhs = jnp.concatenate(split3(col), axis=0)
        part_m += nt_dot(lhs, W[:, :, :, 2 + 4 * c + t].reshape(1024, 128))
        part_r += nt_dot(lhs, RO[4 * c + t])
    part = jnp.concatenate([part_m, part_r], axis=1)
    part = part[0:8] + part[8:16] + part[16:24]
    for j in range(8):
        PB[j] = part[j : j + 1]
    for i, (p, device) in enumerate(zip(ring_peers, ring_devs)):
        send(("p", i), PB.at[p], PR.at[s], device)
    PR[s] = PB[s]
    for i in range(7):
        got(("p", i))
    mixed = jnp.sum(PR[...].reshape(8, D), axis=0, keepdims=True)
    pooled = (xsum + mixed) / count + bout

    img_norm = jnp.sqrt(jnp.sum(pooled * pooled, axis=1, keepdims=True) + NORM_EPS)
    img_unit = pooled / img_norm
    img_b = img_unit.astype(BF16)
    scale = jnp.exp(sc_ref[0:1, 0:1])
    shift = sc_ref[1:2, 0:1]
    texts = jnp.concatenate([TB[0].reshape(256, 640), TB[1].reshape(256, 640)[:, :512]], axis=1)

    def terms(inner, same_label):
        logits = scale * inner + shift
        sign = jnp.where(same_label, 1.0, -1.0)
        neg = -sign * logits
        soft = jnp.maximum(neg, 0.0) + jnp.log1p(jnp.exp(-jnp.abs(neg)))
        return soft, -sign / (1.0 + jnp.exp(-neg))

    inner = nt_dot(jnp.broadcast_to(img_b.astype(F32), (16, D)).astype(BF16), texts)[0:8]
    labels = labl_ref[...]
    lane256 = lax.broadcasted_iota(jnp.int32, (1, 256), 1)
    own_label = jnp.sum(jnp.where(lane256 == v * 16 + u, labels, 0.0), axis=1, keepdims=True)
    soft, grad = terms(inner, labels == own_label)
    stats = [
        jnp.sum(soft[0:1], axis=1, keepdims=True),
        jnp.sum((grad * scale * inner)[0:1], axis=1, keepdims=True),
        jnp.sum(grad[0:1], axis=1, keepdims=True),
    ]
    lane128 = lax.broadcasted_iota(jnp.int32, (1, 128), 1)
    stat_row = sum(jnp.where(lane128 == k, stats[k], 0.0) for k in range(3))
    ICOL[u] = jnp.concatenate([img_b.astype(F32), stat_row], axis=1)
    for i, device in enumerate(col_devs):
        same(("i1", i), ICOL.at[u], device)

    d_img = scale * exact_dot(grad, texts, nn_dot)[0:1]
    d_pooled = (d_img - img_unit * jnp.sum(img_unit * d_img, axis=1, keepdims=True)) / img_norm
    row_grad = d_pooled / count

    GB[s] = row_grad
    for i, device in enumerate(ring_devs):
        same(("g", i), GB.at[s], device)
    for i in range(7):
        got(("g", i))
    grads = GB[...].reshape(8, D).astype(BF16)
    for t in range(5):
        res = nn_dot(grads[:, :1024], W[:, :, :, 2 + 4 * c + t].reshape(1024, 128)) + nn_dot(
            grads[:, 1024:], RO[4 * c + t]
        )
        for j in range(8):
            AB[j, t] = res[j : j + 1]
    for i, (p, device) in enumerate(zip(ring_peers, ring_devs)):
        send(("a", i), AB.at[p], AR.at[s], device)
    AR[s] = AB[s]

    for i in range(15):
        got(("i1", i))
    column = ICOL[...].reshape(16, 1280)
    imgs = column[:, :D].astype(BF16)
    pick = (
        lax.broadcasted_iota(jnp.int32, (16, 256), 1) == 16 * lax.broadcasted_iota(jnp.int32, (16, 256), 0) + u
    )
    texts16 = nn_dot(jnp.where(pick, 1.0, 0.0).astype(BF16), texts).astype(BF16)
    lab2 = lab2_ref[...]
    lab_txt = jnp.sum(
        jnp.where(lax.broadcasted_iota(jnp.int32, (16, 128), 1) == u, lab2, 0.0), axis=1, keepdims=True
    )
    lab_img = jnp.sum(
        jnp.where(lax.broadcasted_iota(jnp.int32, (16, 128), 0) == v, lab2, 0.0), axis=0, keepdims=True
    )[:, :16]
    _, grad_t = terms(nt_dot(texts16, imgs), lab_txt == lab_img)
    d_part = exact_dot(grad_t, imgs, nn_dot)
    col_stats = jnp.sum(column[:, D:], axis=0, keepdims=True)
    for k in range(16):
        DB[k] = jnp.concatenate([d_part[k : k + 1], col_stats], axis=1)
    for i, (p, device) in enumerate(zip(plane_peers, plane_devs)):
        send(("i2", i), DB.at[p], DT.at[v], device)
    DT[v] = DB[v]

    for i in range(7):
        got(("a", i))

    def act_tile(t):
        member = 0
        while member < 7 and first_tile(member + 1) <= t:
            member += 1
        return AR[member, t - first_tile(member)]

    for t in range(NT_IN):
        AF[t] = act_tile(t)

    def bwd(first, count_tiles, main_tiles, start):
        pg = jnp.concatenate([(AF[first + t] * SL[first + t]).astype(BF16) for t in range(count_tiles)], axis=1)
        wm = jnp.concatenate([m.reshape(1024, 128) for m in main_tiles], axis=1)
        wr = jnp.concatenate([RW[first + t] for t in range(count_tiles)], axis=1)
        if start:
            ACC[:, :1024] = nt_dot(pg, wm)
            ACC[:, 1024:] = nt_dot(pg, wr)
        else:
            ACC[:, :1024] += nt_dot(pg, wm)
            ACC[:, 1024:] += nt_dot(pg, wr)

    bwd(32, 2, [W[:, :, :, 0], W[:, :, :, 1]], True)

    @pl.loop(0, 8)
    def _(p):
        q, half = p // 2, p % 2
        bwd(4 * p, 4, [G[:, :, :, q, 5 * half + t] for t in range(4)], False)

    @pl.loop(0, 4)
    def _(i):
        rows = pl.ds(pl.multiple_of(64 * i, 64), 64)
        plain = PLAIN[rows, :]
        q = ACC[rows, :] * VP[0:1, :]
        mean_q = jnp.mean(q, axis=1, keepdims=True)
        mean_qp = jnp.mean(q * plain, axis=1, keepdims=True)
        total = row_grad + RSTD[rows, 0:1] * (q - mean_q - plain * mean_qp)
        ids = (lax.broadcasted_iota(jnp.int32, (64, 1), 0) + 64 * i).astype(F32)
        scaled = jnp.where(ids < count, 256.0 * total, 0.0).astype(BF16)
        out_ref[rows, :] = nt_dot(scaled, PM[...]).astype(BF16)

    for i in range(15):
        got(("i2", i))
    sums = jnp.sum(DT[...].reshape(16, 1280), axis=0, keepdims=True)
    st_ref[...] = sums[:, D:] / 256.0
    d_txt = scale * sums[:, :D]
    unit = TROW[...]
    tg = (d_txt - unit * jnp.sum(unit * d_txt, axis=1, keepdims=True)) / jnp.sqrt(
        jnp.sum(VP[3:4, :] * VP[3:4, :], axis=1, keepdims=True) + NORM_EPS
    )
    tg_ref[...] = nt_dot(jnp.broadcast_to(tg, (16, D)).astype(BF16), PM[...])[0:1].astype(BF16)

    for cp in copies.values():
        cp.wait_send()


def shards(
    patches, counts, norm_gain, norm_bias, weight_in, bias_in, weight_out, bias_out, text_embed, pair_label,
    logit_params,
):
    rows = patches.reshape(ROWS, D)
    wi = jnp.pad(weight_in, ((0, 12), (0, 48)))
    wo = jnp.pad(weight_out, ((0, 48), (0, 0)))
    vec = jnp.concatenate(
        [norm_gain[None], norm_bias[None], bias_out[None], text_embed.astype(F32), jnp.zeros((4, D), F32)], axis=0
    )
    bias = jnp.pad(bias_in, (0, 48)).reshape(NT_IN, 1, 128)
    labels = jnp.transpose(pair_label.reshape(2, 8, 2, 4, 2), (3, 0, 4, 1, 2)).reshape(16, 16).astype(F32)
    scal = jnp.broadcast_to(
        jnp.concatenate([logit_params, counts.reshape(1).astype(F32), jnp.zeros((5,), F32)])[:, None], (8, 128)
    )
    vm = pltpu.VMEM
    scratch = [
        vm((2, 8, 2, 4, 9, 32, 128), BF16),
        vm((2, 8, 2, 13, 32, 128), BF16),
        vm((D, D), BF16),
        vm((ROWS, D), F32),
        vm((ROWS, D), F32),
        vm((ROWS, 128), F32),
        vm((ROWS, D), BF16),
        vm((NT_IN, ROWS, 128), F32),
        vm((NT_IN, 1, 128), F32),
        vm((NT_IN, 1, 128), F32),
        vm((ROWS, D), F32),
        vm((NT_IN, 128, 128), BF16),
        vm((9, 128, 128), BF16),
        vm((1024, 1024), BF16),
        vm((8, D), F32),
        vm((1, D), F32),
        vm((16, 1, 1280), F32),
        vm((2, 16, 16, 640), BF16),
        vm((8, 5, 1, 128), F32),
        vm((8, 1, D), F32),
        vm((8, 1, D), F32),
        vm((8, 1, D), F32),
        vm((8, 5, 1, 128), F32),
        vm((8, 5, 1, 128), F32),
        vm((16, 1, 1280), F32),
        vm((16, 1, 1280), F32),
        vm((16, 1, 1280), F32),
        pltpu.SemaphoreType.DMA((N_COPIES,)),
        pltpu.SemaphoreType.DMA((N_COPIES,)),
    ]
    spec = pl.BlockSpec(memory_space=pltpu.VMEM)
    patch_grad, text_grad, stats = pl.pallas_call(
        kernel,
        out_shape=(
            jax.ShapeDtypeStruct((ROWS, D), BF16),
            jax.ShapeDtypeStruct((1, D), BF16),
            jax.ShapeDtypeStruct((1, 128), F32),
        ),
        in_specs=[spec] * 8,
        out_specs=(spec, spec, spec),
        scratch_shapes=scratch,
        compiler_params=pltpu.CompilerParams(
            collective_id=0, has_side_effects=True, vmem_limit_bytes=56 * 2**20
        ),
    )(rows, wi, wo, vec, bias, labels.reshape(1, 256), jnp.pad(labels, ((0, 0), (0, 112))), scal)
    return patch_grad.reshape(patches.shape), text_grad, stats[0, :3]


def solution(mesh):
    return jax.shard_map(
        shards,
        mesh=mesh,
        in_specs=(
            P("dp", "blk", None, None),
            P("dp", "blk", None),
            P(),
            P(),
            P("dp", None),
            P(),
            P(None, "dp"),
            P(),
            P(("dp", "blk"), None),
            P(),
            P(),
        ),
        out_specs=(P("dp", "blk", None, None), P(("dp", "blk"), None), P()),
        check_vma=False,
    )
```

```python
import jax
import jax.numpy as jnp
from jax import lax
from jax.experimental import pallas as pl
from jax.experimental.pallas import tpu as pltpu
from jax.sharding import PartitionSpec as P

D = 1152
FF = 4304
ROWS = 256
NORM_EPS = 1e-06
GELU_SCALE = 0.7978845608028654
GELU_CUBIC = 0.044715
MESH = pl.DeviceIdType.MESH
F32 = jnp.float32
BF16 = jnp.bfloat16
NT_IN = 34
N_COPIES = 180


def dev(x, y, z, c):
    x, y, z, c = x % 4, y % 4, z % 8, c % 2
    return ((y // 2) * 16 + z * 2 + c, x * 2 + y % 2)


def nt_dot(a, b):
    return lax.dot_general(a, b, (((1,), (1,)), ((), ())), preferred_element_type=F32)


def nn_dot(a, b):
    return jnp.dot(a, b, preferred_element_type=F32)


def split3(v):
    hi = v.astype(BF16)
    rest = v - hi.astype(F32)
    mid = rest.astype(BF16)
    low = (rest - mid.astype(F32)).astype(BF16)
    return hi, mid, low


def exact_dot(v, w, dot):
    rows = v.shape[0]
    hi, mid, low = split3(v)
    res = dot(jnp.concatenate([hi, mid, low], axis=0), w)
    return res[:rows] + res[rows : 2 * rows] + res[2 * rows :]


def rows8(v):
    return jnp.broadcast_to(v, (8, v.shape[1]))


def kernel(
    x_ref, wi_ref, wo_ref, vec_ref, bin_ref, labl_ref, lab2_ref, sc_ref,
    out_ref, tg_ref, st_ref,
    G, W, PM, XP, PLAIN, RSTD, NM, SL, HS, AF, ACC, RW, RO, SF, VP,
    TROW, TCOL, TB, HA, PB, PR, GB, AB, AR, ICOL, DB, DT,
    SS, RS,
):
    dp, blk = lax.axis_index("dp"), lax.axis_index("blk")
    yh, z, c = dp // 16, (dp // 2) % 8, dp % 2
    x, yl = blk // 2, blk % 2
    y = yh * 2 + yl
    cross = dev(x, y + 3 + 2 * yl, z, c)
    share = dev(x, yh * 2 + 1 - yl, z, c)
    partner = dev(x, y, z, c + 1)
    zp, zm = dev(x, y, z + 1, c), dev(x, y, z + 7, c)
    xp, xm = dev(x + 1, y, z, c), dev(x + 3, y, z, c)
    u, v, s = z * 2 + c, x * 4 + y, x * 2 + c
    col_peers = [((u + d) % 16) for d in range(1, 16)]
    col_devs = [dev(x, y, p // 2, p % 2) for p in col_peers]
    plane_peers = [((v + d) % 16) for d in range(1, 16)]
    plane_devs = [dev(p // 4, p % 4, z, c) for p in plane_peers]
    ring_peers = [((s + d) % 8) for d in range(1, 8)]
    ring_devs = [dev(p // 2, y, z, p % 2) for p in ring_peers]

    bar = pltpu.get_barrier_semaphore()
    greet = col_devs + plane_devs + [dev(x + d, y, z, c + 1) for d in (1, 2, 3)]
    greet += [dev(x, y + 3 + 2 * yl, z + d, c) for d in (1, 2, 6, 7)]
    for peer in greet:
        pl.semaphore_signal(bar, inc=1, device_id=peer, device_id_type=MESH)

    copies = {}

    def send(name, src, dst, device):
        k = len(copies)
        cp = pltpu.make_async_remote_copy(
            src_ref=src, dst_ref=dst, send_sem=SS.at[k], recv_sem=RS.at[k], device_id=device, device_id_type=MESH
        )
        cp.start()
        copies[name] = cp

    def same(name, ref, device):
        send(name, ref, ref, device)

    def got(name):
        copies[name].wait_recv()

    def fold(rows, first, count):
        parts = []
        for a in range(0, 8, 2):
            blocks = []
            for b in range(2):
                if a + b < count:
                    t = first + a + b
                    piece = rows[:, 128 * t : 128 * t + 128]
                    blocks.append(pltpu.roll(piece, 4, 0) if b else piece)
            parts.append(sum(blocks) if blocks else jnp.zeros((8, 128), F32))
        return jnp.concatenate(parts, axis=0).astype(BF16)

    wi_tail = wi_ref[32:48, :].astype(F32)[0:8]
    for q in range(4):
        for t in range(8):
            G[yh, 0, c, q, 5 * (t // 4) + t % 4] = wi_ref[0:32, 1024 * q + 128 * t : 1024 * q + 128 * t + 128]
        G[yh, 0, c, q, 4] = fold(wi_tail, 8 * q, 8)
    eye = (
        lax.broadcasted_iota(jnp.int32, (48, 36), 0) == lax.broadcasted_iota(jnp.int32, (48, 36), 1)
    ).astype(F32).astype(BF16)
    wo_first = 8 * x + x // 2
    wo_rows = wo_ref[pl.ds(pl.multiple_of(128 * wo_first, 128), 1152), :]
    wo_t = nt_dot(eye, wo_rows)
    wo_main = wo_t[0:32].astype(BF16)
    for t in range(2):
        W[yh, 0, c, t] = wi_ref[0:32, 4096 + 128 * t : 4096 + 128 * t + 128]
    for t in range(9):
        W[yh, 0, c, 3 + t] = wo_main[:, 128 * t : 128 * t + 128]
    tail = jnp.concatenate([wi_tail[:, 4096:4352], wo_t[32:40]], axis=1)
    W[yh, 0, c, 2] = fold(tail, 0, 8)
    W[yh, 0, c, 12] = fold(tail, 8, 3)

    lane = lax.broadcasted_iota(jnp.int32, (1, D), 1)
    rest = lane - 1024
    place = jnp.where(lane < 1024, lane >> 5, rest >> 2)
    row_in = jnp.where(lane < 1024, lane & 31, 32 + (rest & 3))
    slot = (place >> 1) & 7
    steps = ((slot + 1) >> 1) * (1 - 2 * (slot & 1))
    shard = (place >> 4) * 16 + ((z + 8 + steps) & 7) * 2 + (place & 1)
    natural = 36 * shard + row_in

    @pl.loop(0, 9)
    def _(i):
        first = pl.multiple_of(128 * i, 128)
        rows = lax.broadcasted_iota(jnp.int32, (128, D), 0) + 128 * i
        PM[pl.ds(first, 128), :] = jnp.where(rows == natural, 1.0, 0.0).astype(BF16)

    text_f = vec_ref[3:4, :]
    txt_norm = jnp.sqrt(jnp.sum(text_f * text_f, axis=1, keepdims=True) + NORM_EPS)
    txt_unit = text_f / txt_norm
    TROW[...] = txt_unit
    TCOL[u] = jnp.concatenate([txt_unit.astype(BF16).astype(F32), jnp.zeros((1, 128), F32)], axis=1)

    VP[...] = exact_dot(vec_ref[...], PM[...], nn_dot)
    gain, nbias, bout = VP[0:1, :], VP[1:2, :], VP[2:3, :]
    count = sc_ref[2:3, 0:1]

    @pl.loop(0, 4)
    def _(i):
        rows = pl.ds(pl.multiple_of(64 * i, 64), 64)
        xs = nn_dot(x_ref[rows, :], PM[...])
        XP[rows, :] = xs
        centre = xs - jnp.mean(xs, axis=1, keepdims=True)
        inv = lax.rsqrt(jnp.mean(centre * centre, axis=1, keepdims=True) + NORM_EPS)
        plain = centre * inv
        PLAIN[rows, :] = plain
        RSTD[rows, :] = jnp.broadcast_to(inv, (64, 128))
        NM[rows, :] = (plain * gain + nbias).astype(BF16)

    row_ids = lax.broadcasted_iota(jnp.int32, (ROWS, 1), 0).astype(F32)
    valid = row_ids < count
    xsum = jnp.sum(jnp.where(valid, XP[...], 0.0), axis=0, keepdims=True)

    @pl.loop(0, 8)
    def _(i):
        r = lax.broadcasted_iota(jnp.int32, (128, 1024), 0)
        col = lax.broadcasted_iota(jnp.int32, (128, 1024), 1)
        SF[pl.ds(pl.multiple_of(128 * i, 128), 128), :] = jnp.where(
            col == 32 * (r >> 2) + 4 * i + (r & 3), 1.0, 0.0
        ).astype(BF16)

    pl.semaphore_wait(bar, len(greet))

    other = 1 - yh
    both = slice(None)
    mine5 = pl.ds(4 * yl, 5)
    mine4 = pl.ds(5 * yl, 4)
    slots = [0, pl.ds(1, 2), pl.ds(3, 2), pl.ds(5, 2), 7]

    zpp, zmm = dev(x, y, z + 2, c), dev(x, y, z + 6, c)
    other5 = pl.ds(4 * (1 - yl), 5)

    def z_own(k, device, over):
        send(("zA", k), G.at[yh, 0, c, x, mine5], G.at[yh, k, c, x, mine5], device)
        send(("zB", k), G.at[yh, 0, c, x, other5], G.at[yh, k, c, x, other5], over)

    def z_forward():
        for a in (0, 1):
            send(("zF", 5, a), G.at[a, 3, c, x, mine5], G.at[a, 5, c, x, mine5], zp)
            send(("zF", 6, a), G.at[a, 4, c, x, mine5], G.at[a, 6, c, x, mine5], zm)
        send(("zF", 7), G.at[0, 3, c, x, mine5], G.at[0, 7, c, x, mine5], zpp)
        send(("zF", 8), G.at[1, 4, c, x, mine5], G.at[1, 7, c, x, mine5], zmm)

    chain_r, chain_l = (0, 1, 3, 5, 7), (0, 2, 4, 6, 7)

    part_in, part_out = pl.ds(0, 3), pl.ds(3, 10)

    def w_send(name, sel, src, dst, tiles, device):
        send(name, W.at[sel, src, c, tiles], W.at[sel, dst, c, tiles], device)

    def di_send(n):
        w_send(("iR", n), both if n < 3 else 0, chain_r[n], chain_r[n + 1], part_in, zp)
        w_send(("iL", n), both if n < 3 else 1, chain_l[n], chain_l[n + 1], part_in, zm)

    def di_in(n):
        got(("iR", n - 1))
        got(("iL", n - 1))
        if n < 4:
            di_send(n)

    def d_send(n, a, sel):
        if n < 3 or a == 0:
            w_send(("dR", n, a), sel, chain_r[n], chain_r[n + 1], part_out, zp)
        if n < 3 or a == 1:
            w_send(("dL", n, a), sel, chain_l[n], chain_l[n + 1], part_out, zm)

    def d_in(n, a):
        if n < 4 or a == 0:
            got(("dR", n - 1, a))
        if n < 4 or a == 1:
            got(("dL", n - 1, a))
        if n < 4:
            d_send(n, a, yh if a == 0 else other)

    def d_partner(n):
        same(("pD", n), W.at[:, slots[n], c, part_out], partner)

    def y_send(name, sel, g, q, device):
        same((name, g), G.at[sel, slots[g], c, q % 4, mine4], device)

    def x_send(g):
        sel = other if g == 0 else both
        same(("xR", g), G.at[sel, slots[g], c, x, mine5], xp)
        same(("xL", g), G.at[sel, slots[g], c, x, mine5], xm)
        if g != 0:
            y_send("yA", both, g, x, cross)

    def x_in(g):
        got(("xR", g))
        got(("xL", g))
        sel = other if g == 0 else both
        same(("fR", g), G.at[other if g == 0 else 0, slots[g], c, (x + 3) % 4, mine5], xp)
        if g != 0:
            same(("fL", g), G.at[1, slots[g], c, (x + 1) % 4, mine5], xm)
        y_send("yB", sel, g, x + 3, share)
        y_send("yC", sel, g, x + 1, share)

    def f_in(g):
        got(("fR", g))
        if g != 0:
            got(("fL", g))
            y_send("yD", both, g, x + 2, cross)

    def y_in(g):
        for name in ("yA", "yB", "yC", "yD"):
            got((name, g))
        same(("pG", g), G.at[:, slots[g], c], partner)

    yc = y + 3 + 2 * yl
    z_own(1, zp, dev(x, yc, z + 1, c))
    z_own(2, zm, dev(x, yc, z + 7, c))
    same(("e1",), G.at[yh, 0, c, x, other5], cross)
    z_own(3, zpp, dev(x, yc, z + 2, c))
    z_own(4, zmm, dev(x, yc, z + 6, c))
    same(("i1",), W.at[yh, 0, c, part_in], cross)
    y_send("yA", yh, 0, x, cross)
    y_send("yD", yh, 0, x + 2, cross)
    for i, device in enumerate(col_devs):
        same(("t1", i), TCOL.at[u], device)
    got(("e1",))
    x_send(0)
    got(("i1",))
    for k in (1, 2):
        got(("zA", k))
        got(("zB", k))
    x_send(1)
    for k in (3, 4):
        got(("zA", k))
        got(("zB", k))
    z_forward()
    x_send(2)
    di_send(0)
    same(("d1",), W.at[yh, 0, c, part_out], cross)
    d_send(0, 0, yh)
    x_in(0)
    x_in(1)
    for k in (5, 6):
        for a in (0, 1):
            got(("zF", k, a))
    x_send(3)
    for k in (7, 8):
        got(("zF", k))
    x_send(4)
    di_in(1)
    got(("d1",))
    d_send(0, 1, other)
    x_in(2)
    f_in(0)
    f_in(1)
    d_in(1, 0)
    di_in(2)
    y_in(0)
    x_in(3)
    f_in(2)
    x_in(4)
    d_in(1, 1)
    di_in(3)
    y_in(1)
    f_in(3)
    d_in(2, 0)
    f_in(4)
    y_in(2)
    di_in(4)
    same(("pI",), W.at[:, :, c, part_in], partner)
    d_in(2, 1)
    for i in range(15):
        got(("t1", i))
    block = TCOL[...].reshape(16, 1280).astype(BF16)
    TB[c, v] = jnp.where(c == 0, block[:, :640].astype(F32), block[:, 640:].astype(F32)).astype(BF16)
    y_in(3)
    y_in(4)
    for g in range(3):
        d_partner(g)
    for i, device in enumerate(plane_devs):
        same(("t2", i), TB.at[c, v], device)
    for g in range(5):
        got(("pG", g))
    got(("pI",))

    def unfold(store, pieces):
        res = nn_dot(SF[...], jnp.concatenate([p.reshape(1024, 128) for p in pieces], axis=1)).astype(BF16)
        for j in range(len(pieces)):
            for a in range(8):
                store(j, a, res[128 * a : 128 * a + 128, 128 * j : 128 * j + 128])

    def store_in(base):
        def store(j, a, tile):
            RW[8 * (base + j) + a] = tile
        return store

    def store_direct(j, a, tile, first=0):
        t = first + a
        if t < 2:
            RW[32 + t] = tile
        elif t < 11:
            RO[t - 2] = tile

    for q in (0, 2):
        unfold(store_in(q), [G[:, :, :, q, 4], G[:, :, :, q + 1, 4]])
    unfold(store_direct, [W[:, :, :, 2]])

    def fwd(first, count_tiles, main_tiles):
        wm = jnp.concatenate([m.reshape(1024, 128) for m in main_tiles], axis=1)
        wr = jnp.concatenate([RW[first + t] for t in range(count_tiles)], axis=1)
        pre_all = nn_dot(NM[:, :1024], wm) + nn_dot(NM[:, 1024:], wr)
        for t in range(count_tiles):
            pre = pre_all[:, 128 * t : 128 * t + 128] + bin_ref[first + t]
            sq = pre * pre
            th = jnp.tanh(GELU_SCALE * pre * (1.0 + GELU_CUBIC * sq))
            half = 0.5 * (1.0 + th)
            hid = pre * half
            SL[first + t] = half + 0.5 * pre * (1.0 - th * th) * (GELU_SCALE + 3.0 * GELU_SCALE * GELU_CUBIC * sq)
            HS[first + t] = jnp.sum(jnp.where(valid, hid, 0.0), axis=0, keepdims=True)

    def fwd_pair(start):
        @pl.loop(start, start + 2)
        def _(p):
            q, half = p // 2, p % 2
            fwd(4 * p, 4, [G[:, :, :, q, 5 * half + t] for t in range(4)])

    fwd(32, 2, [W[:, :, :, 0], W[:, :, :, 1]])
    d_in(3, 0)
    fwd_pair(0)
    d_in(3, 1)
    d_partner(3)
    fwd_pair(2)
    d_in(4, 0)
    fwd_pair(4)
    d_in(4, 1)
    d_partner(4)
    fwd_pair(6)

    for g in range(5):
        got(("pD", g))
    unfold(lambda j, a, tile: store_direct(j, a, tile, 8), [W[:, :, :, 12]])
    def first_tile(member):
        return 4 * member + member // 4

    for i in range(15):
        got(("t2", i))
    same(("t3",), TB.at[c], partner)
    for i, (p, device) in enumerate(zip(ring_peers, ring_devs)):
        send(("h", i), HS.at[pl.ds(first_tile(p), 5)], HA.at[s], device)
    HA[s] = HS[pl.ds(first_tile(s), 5)]
    for i in range(7):
        got(("h", i))
    last_mine = jnp.where(s % 4 == 3, 1.0, 0.0)
    part_m = jnp.zeros((24, 1024), F32)
    part_r = jnp.zeros((24, 128), F32)
    for t in range(5):
        col = HA[:, t].reshape(8, 128)
        if t == 4:
            col = col * last_mine
        lhs = jnp.concatenate(split3(col), axis=0)
        part_m += nt_dot(lhs, W[:, :, :, 3 + 4 * c + t].reshape(1024, 128))
        part_r += nt_dot(lhs, RO[4 * c + t])
    part = jnp.concatenate([part_m, part_r], axis=1)
    part = part[0:8] + part[8:16] + part[16:24]
    for j in range(8):
        PB[j] = part[j : j + 1]
    for i, (p, device) in enumerate(zip(ring_peers, ring_devs)):
        send(("p", i), PB.at[p], PR.at[s], device)
    PR[s] = PB[s]
    for i in range(7):
        got(("p", i))
    mixed = jnp.sum(PR[...].reshape(8, D), axis=0, keepdims=True)
    pooled = (xsum + mixed) / count + bout

    got(("t3",))
    texts_nat = jnp.concatenate([TB[0].reshape(256, 640), TB[1].reshape(256, 640)[:, :512]], axis=1)
    texts = nn_dot(texts_nat, PM[...]).astype(BF16)
    img_norm = jnp.sqrt(jnp.sum(pooled * pooled, axis=1, keepdims=True) + NORM_EPS)
    img_unit = pooled / img_norm
    img_b = img_unit.astype(BF16)
    scale = jnp.exp(sc_ref[0:1, 0:1])
    shift = sc_ref[1:2, 0:1]
    def terms(inner, same_label):
        logits = scale * inner + shift
        sign = jnp.where(same_label, 1.0, -1.0)
        neg = -sign * logits
        soft = jnp.maximum(neg, 0.0) + jnp.log1p(jnp.exp(-jnp.abs(neg)))
        return soft, -sign / (1.0 + jnp.exp(-neg))

    img_rows = jnp.broadcast_to(img_b.astype(F32), (16, D)).astype(BF16)
    inner = nt_dot(img_rows, texts)[0:8]
    img_nat = nt_dot(img_rows, PM[...])[0:1]
    labels = labl_ref[...]
    lane256 = lax.broadcasted_iota(jnp.int32, (1, 256), 1)
    own_label = jnp.sum(jnp.where(lane256 == v * 16 + u, labels, 0.0), axis=1, keepdims=True)
    soft, grad = terms(inner, labels == own_label)
    stats = [
        jnp.sum(soft[0:1], axis=1, keepdims=True),
        jnp.sum((grad * scale * inner)[0:1], axis=1, keepdims=True),
        jnp.sum(grad[0:1], axis=1, keepdims=True),
    ]
    lane128 = lax.broadcasted_iota(jnp.int32, (1, 128), 1)
    stat_row = sum(jnp.where(lane128 == k, stats[k], 0.0) for k in range(3))
    ICOL[u] = jnp.concatenate([img_nat, stat_row], axis=1)
    for i, device in enumerate(col_devs):
        same(("i1", i), ICOL.at[u], device)

    d_img = scale * exact_dot(grad, texts, nn_dot)[0:1]
    d_pooled = (d_img - img_unit * jnp.sum(img_unit * d_img, axis=1, keepdims=True)) / img_norm
    row_grad = d_pooled / count

    GB[s] = row_grad
    for i, device in enumerate(ring_devs):
        same(("g", i), GB.at[s], device)
    for i in range(7):
        got(("g", i))
    grads = GB[...].reshape(8, D).astype(BF16)
    for t in range(5):
        res = nn_dot(grads[:, :1024], W[:, :, :, 3 + 4 * c + t].reshape(1024, 128)) + nn_dot(
            grads[:, 1024:], RO[4 * c + t]
        )
        for j in range(8):
            AB[j, t] = res[j : j + 1]
    for i, (p, device) in enumerate(zip(ring_peers, ring_devs)):
        send(("a", i), AB.at[p], AR.at[s], device)
    AR[s] = AB[s]

    for i in range(15):
        got(("i1", i))
    column = ICOL[...].reshape(16, 1280)
    imgs = column[:, :D].astype(BF16)
    pick = (
        lax.broadcasted_iota(jnp.int32, (16, 256), 1) == 16 * lax.broadcasted_iota(jnp.int32, (16, 256), 0) + u
    )
    texts16 = nn_dot(jnp.where(pick, 1.0, 0.0).astype(BF16), texts_nat).astype(BF16)
    lab2 = lab2_ref[...]
    lab_txt = jnp.sum(
        jnp.where(lax.broadcasted_iota(jnp.int32, (16, 128), 1) == u, lab2, 0.0), axis=1, keepdims=True
    )
    lab_img = jnp.sum(
        jnp.where(lax.broadcasted_iota(jnp.int32, (16, 128), 0) == v, lab2, 0.0), axis=0, keepdims=True
    )[:, :16]
    _, grad_t = terms(nt_dot(texts16, imgs), lab_txt == lab_img)
    d_part = exact_dot(grad_t, imgs, nn_dot)
    col_stats = jnp.sum(column[:, D:], axis=0, keepdims=True)
    for k in range(16):
        DB[k] = jnp.concatenate([d_part[k : k + 1], col_stats], axis=1)
    for i, (p, device) in enumerate(zip(plane_peers, plane_devs)):
        send(("i2", i), DB.at[p], DT.at[v], device)
    DT[v] = DB[v]

    for i in range(7):
        got(("a", i))

    def act_tile(t):
        member = 0
        while member < 7 and first_tile(member + 1) <= t:
            member += 1
        return AR[member, t - first_tile(member)]

    for t in range(NT_IN):
        AF[t] = act_tile(t)

    def bwd(first, count_tiles, main_tiles, start):
        pg = jnp.concatenate([(AF[first + t] * SL[first + t]).astype(BF16) for t in range(count_tiles)], axis=1)
        wm = jnp.concatenate([m.reshape(1024, 128) for m in main_tiles], axis=1)
        wr = jnp.concatenate([RW[first + t] for t in range(count_tiles)], axis=1)
        if start:
            ACC[:, :1024] = nt_dot(pg, wm)
            ACC[:, 1024:] = nt_dot(pg, wr)
        else:
            ACC[:, :1024] += nt_dot(pg, wm)
            ACC[:, 1024:] += nt_dot(pg, wr)

    bwd(32, 2, [W[:, :, :, 0], W[:, :, :, 1]], True)

    @pl.loop(0, 8)
    def _(p):
        q, half = p // 2, p % 2
        bwd(4 * p, 4, [G[:, :, :, q, 5 * half + t] for t in range(4)], False)

    @pl.loop(0, 4)
    def _(i):
        rows = pl.ds(pl.multiple_of(64 * i, 64), 64)
        plain = PLAIN[rows, :]
        q = ACC[rows, :] * VP[0:1, :]
        mean_q = jnp.mean(q, axis=1, keepdims=True)
        mean_qp = jnp.mean(q * plain, axis=1, keepdims=True)
        total = row_grad + RSTD[rows, 0:1] * (q - mean_q - plain * mean_qp)
        ids = (lax.broadcasted_iota(jnp.int32, (64, 1), 0) + 64 * i).astype(F32)
        scaled = jnp.where(ids < count, 256.0 * total, 0.0).astype(BF16)
        out_ref[rows, :] = nt_dot(scaled, PM[...]).astype(BF16)

    for i in range(15):
        got(("i2", i))
    sums = jnp.sum(DT[...].reshape(16, 1280), axis=0, keepdims=True)
    st_ref[...] = sums[:, D:] / 256.0
    d_txt = scale * sums[:, :D]
    unit = TROW[...]
    tg = (d_txt - unit * jnp.sum(unit * d_txt, axis=1, keepdims=True)) / jnp.sqrt(
        jnp.sum(vec_ref[3:4, :] * vec_ref[3:4, :], axis=1, keepdims=True) + NORM_EPS
    )
    tg_ref[...] = tg.astype(BF16)

    for cp in copies.values():
        cp.wait_send()


def shards(
    patches, counts, norm_gain, norm_bias, weight_in, bias_in, weight_out, bias_out, text_embed, pair_label,
    logit_params,
):
    rows = patches.reshape(ROWS, D)
    wi = jnp.pad(weight_in, ((0, 12), (0, 48)))
    wo = jnp.pad(weight_out, ((0, 48), (0, 0)))
    vec = jnp.concatenate(
        [norm_gain[None], norm_bias[None], bias_out[None], text_embed.astype(F32), jnp.zeros((4, D), F32)], axis=0
    )
    bias = jnp.pad(bias_in, (0, 48)).reshape(NT_IN, 1, 128)
    labels = jnp.transpose(pair_label.reshape(2, 8, 2, 4, 2), (3, 0, 4, 1, 2)).reshape(16, 16).astype(F32)
    scal = jnp.broadcast_to(
        jnp.concatenate([logit_params, counts.reshape(1).astype(F32), jnp.zeros((5,), F32)])[:, None], (8, 128)
    )
    vm = pltpu.VMEM
    scratch = [
        vm((2, 8, 2, 4, 9, 32, 128), BF16),
        vm((2, 8, 2, 13, 32, 128), BF16),
        vm((D, D), BF16),
        vm((ROWS, D), F32),
        vm((ROWS, D), F32),
        vm((ROWS, 128), F32),
        vm((ROWS, D), BF16),
        vm((NT_IN, ROWS, 128), F32),
        vm((NT_IN, 1, 128), F32),
        vm((NT_IN, 1, 128), F32),
        vm((ROWS, D), F32),
        vm((NT_IN, 128, 128), BF16),
        vm((9, 128, 128), BF16),
        vm((1024, 1024), BF16),
        vm((8, D), F32),
        vm((1, D), F32),
        vm((16, 1, 1280), F32),
        vm((2, 16, 16, 640), BF16),
        vm((8, 5, 1, 128), F32),
        vm((8, 1, D), F32),
        vm((8, 1, D), F32),
        vm((8, 1, D), F32),
        vm((8, 5, 1, 128), F32),
        vm((8, 5, 1, 128), F32),
        vm((16, 1, 1280), F32),
        vm((16, 1, 1280), F32),
        vm((16, 1, 1280), F32),
        pltpu.SemaphoreType.DMA((N_COPIES,)),
        pltpu.SemaphoreType.DMA((N_COPIES,)),
    ]
    spec = pl.BlockSpec(memory_space=pltpu.VMEM)
    patch_grad, text_grad, stats = pl.pallas_call(
        kernel,
        out_shape=(
            jax.ShapeDtypeStruct((ROWS, D), BF16),
            jax.ShapeDtypeStruct((1, D), BF16),
            jax.ShapeDtypeStruct((1, 128), F32),
        ),
        in_specs=[spec] * 8,
        out_specs=(spec, spec, spec),
        scratch_shapes=scratch,
        compiler_params=pltpu.CompilerParams(
            collective_id=0, has_side_effects=True, vmem_limit_bytes=56 * 2**20
        ),
    )(rows, wi, wo, vec, bias, labels.reshape(1, 256), jnp.pad(labels, ((0, 0), (0, 112))), scal)
    return patch_grad.reshape(patches.shape), text_grad, stats[0, :3]


def solution(mesh):
    return jax.shard_map(
        shards,
        mesh=mesh,
        in_specs=(
            P("dp", "blk", None, None),
            P("dp", "blk", None),
            P(),
            P(),
            P("dp", None),
            P(),
            P(None, "dp"),
            P(),
            P(("dp", "blk"), None),
            P(),
            P(),
        ),
        out_specs=(P("dp", "blk", None, None), P(("dp", "blk"), None), P()),
        check_vma=False,
    )
```

```python
import jax
import jax.numpy as jnp
from jax import lax
from jax.experimental import pallas as pl
from jax.experimental.pallas import tpu as pltpu
from jax.sharding import PartitionSpec as P

D = 1152
FF = 4304
ROWS = 256
NORM_EPS = 1e-06
GELU_SCALE = 0.7978845608028654
GELU_CUBIC = 0.044715
MESH = pl.DeviceIdType.MESH
F32 = jnp.float32
BF16 = jnp.bfloat16
NT_IN = 34
N_COPIES = 240


def dev(x, y, z, c):
    x, y, z, c = x % 4, y % 4, z % 8, c % 2
    return ((y // 2) * 16 + z * 2 + c, x * 2 + y % 2)


def nt_dot(a, b):
    return lax.dot_general(a, b, (((1,), (1,)), ((), ())), preferred_element_type=F32)


def nn_dot(a, b):
    return jnp.dot(a, b, preferred_element_type=F32)


def split3(v):
    hi = v.astype(BF16)
    rest = v - hi.astype(F32)
    mid = rest.astype(BF16)
    low = (rest - mid.astype(F32)).astype(BF16)
    return hi, mid, low


def exact_dot(v, w, dot):
    rows = v.shape[0]
    hi, mid, low = split3(v)
    res = dot(jnp.concatenate([hi, mid, low], axis=0), w)
    return res[:rows] + res[rows : 2 * rows] + res[2 * rows :]


def rows8(v):
    return jnp.broadcast_to(v, (8, v.shape[1]))


def kernel(
    x_ref, wi_in, wo_in, vec_in, text_in, lab_in, lp_ref, cnt_ref,
    out_ref, tg_ref, st_ref,
    G, W, PM, XP, PLAIN, RSTD, NM, SL, HS, AF, ACC, RW, RO, SF, VP,
    TROW, TCOL, TB, HA, PB, PR, GB, AB, AR, ICOL, DB, DT,
    WS, BS, VEC,
    SS, RS,
):
    dp, blk = lax.axis_index("dp"), lax.axis_index("blk")
    yh, z, c = dp // 16, (dp // 2) % 8, dp % 2
    x, yl = blk // 2, blk % 2
    y = yh * 2 + yl
    cross = dev(x, y + 3 + 2 * yl, z, c)
    share = dev(x, yh * 2 + 1 - yl, z, c)
    partner = dev(x, y, z, c + 1)
    zp, zm = dev(x, y, z + 1, c), dev(x, y, z + 7, c)
    xp, xm = dev(x + 1, y, z, c), dev(x + 3, y, z, c)
    u, v, s = z * 2 + c, x * 4 + y, x * 2 + c
    col_peers = [((u + d) % 16) for d in range(1, 16)]
    col_devs = [dev(x, y, p // 2, p % 2) for p in col_peers]
    plane_peers = [((v + d) % 16) for d in range(1, 16)]
    plane_devs = [dev(p // 4, p % 4, z, c) for p in plane_peers]
    ring_peers = [((s + d) % 8) for d in range(1, 8)]
    ring_devs = [dev(p // 2, y, z, p % 2) for p in ring_peers]

    bar = pltpu.get_barrier_semaphore()
    greet = col_devs + plane_devs + [dev(x + d, y, z, c + 1) for d in (1, 2, 3)]
    greet += [dev(x, y + 3 + 2 * yl, z + d, c) for d in (1, 2, 6, 7)]
    for peer in greet:
        pl.semaphore_signal(bar, inc=1, device_id=peer, device_id_type=MESH)

    copies = {}

    def send(name, src, dst, device):
        k = len(copies)
        cp = pltpu.make_async_remote_copy(
            src_ref=src, dst_ref=dst, send_sem=SS.at[k], recv_sem=RS.at[k], device_id=device, device_id_type=MESH
        )
        cp.start()
        copies[name] = cp

    def same(name, ref, device):
        send(name, ref, ref, device)

    def got(name):
        copies[name].wait_recv()

    def fold(rows, first, count):
        parts = []
        for a in range(0, 8, 2):
            blocks = []
            for b in range(2):
                if a + b < count:
                    t = first + a + b
                    piece = rows[:, 128 * t : 128 * t + 128]
                    blocks.append(pltpu.roll(piece, 4, 0) if b else piece)
            parts.append(sum(blocks) if blocks else jnp.zeros((8, 128), F32))
        return jnp.concatenate(parts, axis=0).astype(BF16)

    for k, w_ref in ((0, wi_in), (1, wo_in)):
        WS[k, :, 4224:4352] = jnp.zeros((48, 128), BF16)
        WS[k, 32:48, :] = jnp.zeros((16, 4352), BF16)
        WS[k, 0:32, 0:FF] = w_ref[0:32, :]
        WS[k, 32:36, 0:FF] = w_ref[32:36, :]
    wi_ref, wo_ref = WS.at[0], WS.at[1]
    BS[:, 4224:4352] = jnp.zeros((1, 128), F32)
    BS[:, 0:FF] = vec_in[:, 3 * D :]
    VEC[...] = jnp.zeros((8, D), F32)
    VEC[0:1, :] = vec_in[:, 0 * D : 1 * D]
    VEC[1:2, :] = vec_in[:, 1 * D : 2 * D]
    VEC[2:3, :] = vec_in[:, 2 * D : 3 * D]
    VEC[3:4, :] = text_in[...].astype(F32)
    wi_tail = wi_ref[32:48, :].astype(F32)[0:8]
    for q in range(4):
        for t in range(8):
            G[yh, 0, c, q, 5 * (t // 4) + t % 4] = wi_ref[0:32, 1024 * q + 128 * t : 1024 * q + 128 * t + 128]
        G[yh, 0, c, q, 4] = fold(wi_tail, 8 * q, 8)
    wo_first = 8 * x + x // 2
    wo_cols = pl.ds(pl.multiple_of(128 * wo_first, 128), 1152)
    wo_main = wo_ref[0:32, wo_cols]
    wo_tail = wo_ref[32:48, wo_cols].astype(F32)[0:8]
    for t in range(2):
        W[yh, 0, c, t] = wi_ref[0:32, 4096 + 128 * t : 4096 + 128 * t + 128]
    for t in range(9):
        W[yh, 0, c, 3 + t] = wo_main[:, 128 * t : 128 * t + 128]
    tail = jnp.concatenate([wi_tail[:, 4096:4352], wo_tail], axis=1)
    W[yh, 0, c, 2] = fold(tail, 0, 8)
    W[yh, 0, c, 12] = fold(tail, 8, 3)

    pl.semaphore_wait(bar, len(greet))

    other = 1 - yh
    both = slice(None)
    mine5 = pl.ds(4 * yl, 5)
    mine4 = pl.ds(5 * yl, 4)
    slots = [0, pl.ds(1, 2), pl.ds(3, 2), pl.ds(5, 2), 7]

    zpp, zmm = dev(x, y, z + 2, c), dev(x, y, z + 6, c)
    other5 = pl.ds(4 * (1 - yl), 5)

    def z_own(k, device, over):
        send(("zA", k), G.at[yh, 0, c, x, mine5], G.at[yh, k, c, x, mine5], device)
        send(("zB", k), G.at[yh, 0, c, x, other5], G.at[yh, k, c, x, other5], over)

    def z_forward():
        for a in (0, 1):
            send(("zF", 5, a), G.at[a, 3, c, x, mine5], G.at[a, 5, c, x, mine5], zp)
            send(("zF", 6, a), G.at[a, 4, c, x, mine5], G.at[a, 6, c, x, mine5], zm)
        send(("zF", 7), G.at[0, 3, c, x, mine5], G.at[0, 7, c, x, mine5], zpp)
        send(("zF", 8), G.at[1, 4, c, x, mine5], G.at[1, 7, c, x, mine5], zmm)

    chain_r, chain_l = (0, 1, 3, 5, 7), (0, 2, 4, 6, 7)

    part_in, part_out = pl.ds(0, 3), pl.ds(3, 10)

    def w_send(name, sel, src, dst, tiles, device):
        send(name, W.at[sel, src, c, tiles], W.at[sel, dst, c, tiles], device)

    def di_send(n):
        w_send(("iR", n), both if n < 3 else 0, chain_r[n], chain_r[n + 1], part_in, zp)
        w_send(("iL", n), both if n < 3 else 1, chain_l[n], chain_l[n + 1], part_in, zm)

    def di_in(n):
        got(("iR", n - 1))
        got(("iL", n - 1))
        if n < 4:
            di_send(n)

    def d_send(n, a, sel):
        if n < 3 or a == 0:
            w_send(("dR", n, a), sel, chain_r[n], chain_r[n + 1], part_out, zp)
        if n < 3 or a == 1:
            w_send(("dL", n, a), sel, chain_l[n], chain_l[n + 1], part_out, zm)

    def d_in(n, a):
        if n < 4 or a == 0:
            got(("dR", n - 1, a))
        if n < 4 or a == 1:
            got(("dL", n - 1, a))
        if n < 4:
            d_send(n, a, yh if a == 0 else other)

    def d_partner(n):
        same(("pD", n), W.at[:, slots[n], c, part_out], partner)

    def y_send(name, sel, g, q, device):
        same((name, g), G.at[sel, slots[g], c, q % 4, mine4], device)

    def x_send(g):
        sel = other if g == 0 else both
        same(("xR", g), G.at[sel, slots[g], c, x, mine5], xp)
        same(("xL", g), G.at[sel, slots[g], c, x, mine5], xm)
        if g != 0:
            y_send("yA", both, g, x, cross)

    def x_in(g):
        got(("xR", g))
        got(("xL", g))
        sel = other if g == 0 else both
        same(("fR", g), G.at[other if g == 0 else 0, slots[g], c, (x + 3) % 4, mine5], xp)
        if g != 0:
            same(("fL", g), G.at[1, slots[g], c, (x + 1) % 4, mine5], xm)
        y_send("yB", sel, g, x + 3, share)
        y_send("yC", sel, g, x + 1, share)

    def f_in(g):
        got(("fR", g))
        if g != 0:
            got(("fL", g))
            y_send("yD", both, g, x + 2, cross)
        same(("pF", g), G.at[:, slots[g], c, :, mine5], partner)

    def y_in(g):
        for name in ("yA", "yB", "yC", "yD"):
            got((name, g))
        same(("pG", g), G.at[:, slots[g], c, :, pl.ds(5 * (1 - yl), 4)], partner)

    yc = y + 3 + 2 * yl
    z_own(1, zp, dev(x, yc, z + 1, c))
    z_own(2, zm, dev(x, yc, z + 7, c))
    same(("e1",), G.at[yh, 0, c, x, other5], cross)
    text_f = VEC[3:4, :]
    txt_norm = jnp.sqrt(jnp.sum(text_f * text_f, axis=1, keepdims=True) + NORM_EPS)
    txt_unit = text_f / txt_norm
    TROW[...] = txt_unit
    TCOL[u] = jnp.concatenate([txt_unit.astype(BF16).astype(F32), jnp.zeros((1, 128), F32)], axis=1)

    for i, device in enumerate(col_devs):
        same(("t1", i), TCOL.at[u], device)
    z_own(3, zpp, dev(x, yc, z + 2, c))
    z_own(4, zmm, dev(x, yc, z + 6, c))
    same(("i1",), W.at[yh, 0, c, part_in], cross)
    y_send("yA", yh, 0, x, cross)
    y_send("yD", yh, 0, x + 2, cross)
    lane = lax.broadcasted_iota(jnp.int32, (1, D), 1)
    rest = lane - 1024
    place = jnp.where(lane < 1024, lane >> 5, rest >> 2)
    row_in = jnp.where(lane < 1024, lane & 31, 32 + (rest & 3))
    slot = (place >> 1) & 7
    steps = ((slot + 1) >> 1) * (1 - 2 * (slot & 1))
    shard = (place >> 4) * 16 + ((z + 8 + steps) & 7) * 2 + (place & 1)
    natural = 36 * shard + row_in

    @pl.loop(0, 9)
    def _(i):
        first = pl.multiple_of(128 * i, 128)
        rows = lax.broadcasted_iota(jnp.int32, (128, D), 0) + 128 * i
        PM[pl.ds(first, 128), :] = jnp.where(rows == natural, 1.0, 0.0).astype(BF16)

    got(("e1",))
    x_send(0)
    got(("i1",))
    VP[...] = exact_dot(VEC[...], PM[...], nn_dot)
    gain, nbias, bout = VP[0:1, :], VP[1:2, :], VP[2:3, :]
    count = jnp.zeros((1, 128), F32)[:, 0:1] + cnt_ref[0].astype(F32)

    for k in (1, 2):
        got(("zA", k))
        got(("zB", k))
    x_send(1)
    for k in (3, 4):
        got(("zA", k))
        got(("zB", k))
    z_forward()
    x_send(2)
    di_send(0)
    same(("d1",), W.at[yh, 0, c, part_out], cross)
    d_send(0, 0, yh)
    x_in(0)
    @pl.loop(0, 4)
    def _(i):
        rows = pl.ds(pl.multiple_of(64 * i, 64), 64)
        xs = nn_dot(x_ref[rows, :], PM[...])
        XP[rows, :] = xs
        centre = xs - jnp.mean(xs, axis=1, keepdims=True)
        inv = lax.rsqrt(jnp.mean(centre * centre, axis=1, keepdims=True) + NORM_EPS)
        plain = centre * inv
        PLAIN[rows, :] = plain
        RSTD[rows, :] = jnp.broadcast_to(inv, (64, 128))
        NM[rows, :] = (plain * gain + nbias).astype(BF16)

    x_in(1)
    for k in (5, 6):
        for a in (0, 1):
            got(("zF", k, a))
    x_send(3)
    for k in (7, 8):
        got(("zF", k))
    x_send(4)
    di_in(1)
    row_ids = lax.broadcasted_iota(jnp.int32, (ROWS, 1), 0).astype(F32)
    valid = row_ids < count
    xsum = jnp.sum(jnp.where(valid, XP[...], 0.0), axis=0, keepdims=True)

    got(("d1",))
    d_send(0, 1, other)
    x_in(2)
    f_in(0)
    f_in(1)
    d_in(1, 0)
    di_in(2)
    y_in(0)
    @pl.loop(0, 8)
    def _(i):
        r = lax.broadcasted_iota(jnp.int32, (128, 1024), 0)
        col = lax.broadcasted_iota(jnp.int32, (128, 1024), 1)
        SF[pl.ds(pl.multiple_of(128 * i, 128), 128), :] = jnp.where(
            col == 32 * (r >> 2) + 4 * i + (r & 3), 1.0, 0.0
        ).astype(BF16)

    x_in(3)
    f_in(2)
    x_in(4)
    d_in(1, 1)
    di_in(3)
    y_in(1)
    labels_nat = jnp.broadcast_to(lab_in[...].astype(F32), (16, 256))

    def natural_pair(v_, u_):
        return ((((v_ >> 1) & 1) * 16 + u_) * 8) + ((v_ >> 2) * 2) + (v_ & 1)

    row256 = lax.broadcasted_iota(jnp.int32, (256, 256), 0)
    col256 = lax.broadcasted_iota(jnp.int32, (256, 256), 1)
    labels_b = labels_nat.astype(BF16)
    labels = nn_dot(labels_b, jnp.where(row256 == natural_pair(col256 >> 4, col256 & 15), 1.0, 0.0).astype(BF16))[0:1]
    own_label = jnp.sum(jnp.where(col256[0:1] == v * 16 + u, labels, 0.0), axis=1, keepdims=True)
    lab_img = nn_dot(
        labels_b, jnp.where(row256[:, :128] == natural_pair(v, col256[:, :128] & 15), 1.0, 0.0).astype(BF16)
    )[0:1, :16]
    lab_txt = jnp.sum(
        jnp.where(col256[:16] == natural_pair(row256[:16], u), labels_nat, 0.0), axis=1, keepdims=True
    )

    f_in(3)
    d_in(2, 0)
    f_in(4)
    y_in(2)
    di_in(4)
    same(("pI",), W.at[:, :, c, part_in], partner)
    d_in(2, 1)
    for i in range(15):
        got(("t1", i))
    block = TCOL[...].reshape(16, 1280).astype(BF16)
    TB[c, v] = jnp.where(c == 0, block[:, :640].astype(F32), block[:, 640:].astype(F32)).astype(BF16)
    def unfold(store, pieces):
        res = nn_dot(SF[...], jnp.concatenate([p.reshape(1024, 128) for p in pieces], axis=1)).astype(BF16)
        for j in range(len(pieces)):
            for a in range(8):
                store(j, a, res[128 * a : 128 * a + 128, 128 * j : 128 * j + 128])

    def store_in(base):
        def store(j, a, tile):
            RW[8 * (base + j) + a] = tile
        return store

    def store_direct(j, a, tile, first=0):
        t = first + a
        if t < 2:
            RW[32 + t] = tile
        elif t < 11:
            RO[t - 2] = tile

    def fwd(first, count_tiles, main_tiles):
        wm = jnp.concatenate([m.reshape(1024, 128) for m in main_tiles], axis=1)
        wr = jnp.concatenate([RW[first + t] for t in range(count_tiles)], axis=1)
        pre_all = nn_dot(NM[:, :1024], wm) + nn_dot(NM[:, 1024:], wr)
        bias = BS[:, pl.ds(pl.multiple_of(128 * first, 128), 128 * count_tiles)]
        for t in range(count_tiles):
            pre = pre_all[:, 128 * t : 128 * t + 128] + bias[:, 128 * t : 128 * t + 128]
            sq = pre * pre
            th = jnp.tanh(GELU_SCALE * pre * (1.0 + GELU_CUBIC * sq))
            half = 0.5 * (1.0 + th)
            hid = pre * half
            SL[first + t] = half + 0.5 * pre * (1.0 - th * th) * (GELU_SCALE + 3.0 * GELU_SCALE * GELU_CUBIC * sq)
            HS[first + t] = jnp.sum(jnp.where(valid, hid, 0.0), axis=0, keepdims=True)

    def fwd_pair(start):
        @pl.loop(start, start + 2)
        def _(p):
            q, half = p // 2, p % 2
            fwd(4 * p, 4, [G[:, :, :, q, 5 * half + t] for t in range(4)])

    y_in(3)
    for g in range(5):
        got(("pF", g))
    got(("pI",))
    for q in (0, 2):
        unfold(store_in(q), [G[:, :, :, q, 4], G[:, :, :, q + 1, 4]])
    unfold(store_direct, [W[:, :, :, 2]])

    y_in(4)
    for g in range(3):
        d_partner(g)
    for i, device in enumerate(plane_devs):
        same(("t2", i), TB.at[c, v], device)
    fwd(32, 2, [W[:, :, :, 0], W[:, :, :, 1]])
    for g in range(5):
        got(("pG", g))

    d_in(3, 0)
    fwd_pair(0)
    d_in(3, 1)
    d_partner(3)
    fwd_pair(2)
    d_in(4, 0)
    fwd_pair(4)
    d_in(4, 1)
    d_partner(4)
    fwd_pair(6)

    def first_tile(member):
        return 4 * member + member // 4

    for i, (p, device) in enumerate(zip(ring_peers, ring_devs)):
        send(("h", i), HS.at[pl.ds(first_tile(p), 5)], HA.at[s], device)
    HA[s] = HS[pl.ds(first_tile(s), 5)]
    for i in range(15):
        got(("t2", i))
    same(("t3",), TB.at[c], partner)
    for g in range(5):
        got(("pD", g))
    unfold(lambda j, a, tile: store_direct(j, a, tile, 8), [W[:, :, :, 12]])
    for i in range(7):
        got(("h", i))
    last_mine = jnp.where(s % 4 == 3, 1.0, 0.0)
    part_m = jnp.zeros((24, 1024), F32)
    part_r = jnp.zeros((24, 128), F32)
    for t in range(5):
        col = HA[:, t].reshape(8, 128)
        if t == 4:
            col = col * last_mine
        lhs = jnp.concatenate(split3(col), axis=0)
        part_m += nt_dot(lhs, W[:, :, :, 3 + 4 * c + t].reshape(1024, 128))
        part_r += nt_dot(lhs, RO[4 * c + t])
    part = jnp.concatenate([part_m, part_r], axis=1)
    part = part[0:8] + part[8:16] + part[16:24]
    for j in range(8):
        PB[j] = part[j : j + 1]
    for i, (p, device) in enumerate(zip(ring_peers, ring_devs)):
        send(("p", i), PB.at[p], PR.at[s], device)
    PR[s] = PB[s]
    got(("t3",))
    texts_nat = jnp.concatenate([TB[0].reshape(256, 640), TB[1].reshape(256, 640)[:, :512]], axis=1)
    texts = nn_dot(texts_nat, PM[...]).astype(BF16)
    for i in range(7):
        got(("p", i))
    mixed = jnp.sum(PR[...].reshape(8, D), axis=0, keepdims=True)
    pooled = (xsum + mixed) / count + bout

    img_norm = jnp.sqrt(jnp.sum(pooled * pooled, axis=1, keepdims=True) + NORM_EPS)
    img_unit = pooled / img_norm
    img_b = img_unit.astype(BF16)
    scale = jnp.exp(jnp.zeros((1, 128), F32) + lp_ref[0])[:, 0:1]
    shift = lp_ref[1]
    def terms(inner, same_label):
        logits = scale * inner + shift
        sign = jnp.where(same_label, 1.0, -1.0)
        neg = -sign * logits
        soft = jnp.maximum(neg, 0.0) + jnp.log1p(jnp.exp(-jnp.abs(neg)))
        return soft, -sign / (1.0 + jnp.exp(-neg))

    img_rows = jnp.broadcast_to(img_b.astype(F32), (16, D)).astype(BF16)
    inner = nt_dot(img_rows, texts)[0:8]
    soft, grad = terms(inner, labels == own_label)
    d_img = scale * exact_dot(grad, texts, nn_dot)[0:1]
    d_pooled = (d_img - img_unit * jnp.sum(img_unit * d_img, axis=1, keepdims=True)) / img_norm
    row_grad = d_pooled / count

    GB[s] = row_grad
    for i, device in enumerate(ring_devs):
        same(("g", i), GB.at[s], device)
    stats = [
        jnp.sum(soft[0:1], axis=1, keepdims=True),
        jnp.sum((grad * scale * inner)[0:1], axis=1, keepdims=True),
        jnp.sum(grad[0:1], axis=1, keepdims=True),
    ]
    lane128 = lax.broadcasted_iota(jnp.int32, (1, 128), 1)
    stat_row = sum(jnp.where(lane128 == k, stats[k], 0.0) for k in range(3))
    img_nat = nt_dot(img_rows, PM[...])[0:1]
    ICOL[u] = jnp.concatenate([img_nat, stat_row], axis=1)
    for i, device in enumerate(col_devs):
        same(("i1", i), ICOL.at[u], device)
    for i in range(7):
        got(("g", i))
    grads = GB[...].reshape(8, D).astype(BF16)
    for t in range(5):
        res = nn_dot(grads[:, :1024], W[:, :, :, 3 + 4 * c + t].reshape(1024, 128)) + nn_dot(
            grads[:, 1024:], RO[4 * c + t]
        )
        for j in range(8):
            AB[j, t] = res[j : j + 1]
    for i, (p, device) in enumerate(zip(ring_peers, ring_devs)):
        send(("a", i), AB.at[p], AR.at[s], device)
    AR[s] = AB[s]

    for i in range(15):
        got(("i1", i))
    column = ICOL[...].reshape(16, 1280)
    imgs = column[:, :D].astype(BF16)
    pick = (
        lax.broadcasted_iota(jnp.int32, (16, 256), 1) == 16 * lax.broadcasted_iota(jnp.int32, (16, 256), 0) + u
    )
    texts16 = nn_dot(jnp.where(pick, 1.0, 0.0).astype(BF16), texts_nat).astype(BF16)
    _, grad_t = terms(nt_dot(texts16, imgs), lab_txt == lab_img)
    d_part = exact_dot(grad_t, imgs, nn_dot)
    col_stats = jnp.sum(column[:, D:], axis=0, keepdims=True)
    for k in range(16):
        DB[k] = jnp.concatenate([d_part[k : k + 1], col_stats], axis=1)
    for i, (p, device) in enumerate(zip(plane_peers, plane_devs)):
        send(("i2", i), DB.at[p], DT.at[v], device)
    DT[v] = DB[v]

    for i in range(7):
        got(("a", i))

    def act_tile(t):
        member = 0
        while member < 7 and first_tile(member + 1) <= t:
            member += 1
        return AR[member, t - first_tile(member)]

    for t in range(NT_IN):
        AF[t] = act_tile(t)

    def bwd(first, count_tiles, main_tiles, start):
        pg = jnp.concatenate([(AF[first + t] * SL[first + t]).astype(BF16) for t in range(count_tiles)], axis=1)
        wm = jnp.concatenate([m.reshape(1024, 128) for m in main_tiles], axis=1)
        wr = jnp.concatenate([RW[first + t] for t in range(count_tiles)], axis=1)
        if start:
            ACC[:, :1024] = nt_dot(pg, wm)
            ACC[:, 1024:] = nt_dot(pg, wr)
        else:
            ACC[:, :1024] += nt_dot(pg, wm)
            ACC[:, 1024:] += nt_dot(pg, wr)

    bwd(32, 2, [W[:, :, :, 0], W[:, :, :, 1]], True)

    @pl.loop(0, 8)
    def _(p):
        q, half = p // 2, p % 2
        bwd(4 * p, 4, [G[:, :, :, q, 5 * half + t] for t in range(4)], False)

    @pl.loop(0, 4)
    def _(i):
        rows = pl.ds(pl.multiple_of(64 * i, 64), 64)
        plain = PLAIN[rows, :]
        q = ACC[rows, :] * VP[0:1, :]
        mean_q = jnp.mean(q, axis=1, keepdims=True)
        mean_qp = jnp.mean(q * plain, axis=1, keepdims=True)
        total = row_grad + RSTD[rows, 0:1] * (q - mean_q - plain * mean_qp)
        ids = (lax.broadcasted_iota(jnp.int32, (64, 1), 0) + 64 * i).astype(F32)
        scaled = jnp.where(ids < count, 256.0 * total, 0.0).astype(BF16)
        out_ref[rows, :] = nt_dot(scaled, PM[...]).astype(BF16)

    for i in range(15):
        got(("i2", i))
    sums = jnp.sum(DT[...].reshape(16, 1280), axis=0, keepdims=True)
    for k in range(3):
        st_ref[k] = jnp.sum(jnp.where(lane128 == k, sums[:, D:], 0.0)) / 256.0
    d_txt = scale * sums[:, :D]
    unit = TROW[...]
    tg = (d_txt - unit * jnp.sum(unit * d_txt, axis=1, keepdims=True)) / jnp.sqrt(
        jnp.sum(VEC[3:4, :] * VEC[3:4, :], axis=1, keepdims=True) + NORM_EPS
    )
    tg_ref[...] = tg.astype(BF16)

    for cp in copies.values():
        cp.wait_send()


def shards(
    patches, counts, norm_gain, norm_bias, weight_in, bias_in, weight_out, bias_out, text_embed, pair_label,
    logit_params,
):
    vm = pltpu.VMEM
    scratch = [
        vm((2, 8, 2, 4, 9, 32, 128), BF16),
        vm((2, 8, 2, 13, 32, 128), BF16),
        vm((D, D), BF16),
        vm((ROWS, D), F32),
        vm((ROWS, D), F32),
        vm((ROWS, 128), F32),
        vm((ROWS, D), BF16),
        vm((NT_IN, ROWS, 128), F32),
        vm((NT_IN, 1, 128), F32),
        vm((NT_IN, 1, 128), F32),
        vm((ROWS, D), F32),
        vm((NT_IN, 128, 128), BF16),
        vm((9, 128, 128), BF16),
        vm((1024, 1024), BF16),
        vm((8, D), F32),
        vm((1, D), F32),
        vm((16, 1, 1280), F32),
        vm((2, 16, 16, 640), BF16),
        vm((8, 5, 1, 128), F32),
        vm((8, 1, D), F32),
        vm((8, 1, D), F32),
        vm((8, 1, D), F32),
        vm((8, 5, 1, 128), F32),
        vm((8, 5, 1, 128), F32),
        vm((16, 1, 1280), F32),
        vm((16, 1, 1280), F32),
        vm((16, 1, 1280), F32),
        vm((2, 48, 4352), BF16),
        vm((1, 4352), F32),
        vm((8, D), F32),
        pltpu.SemaphoreType.DMA((N_COPIES,)),
        pltpu.SemaphoreType.DMA((N_COPIES,)),
    ]
    spec = pl.BlockSpec(memory_space=pltpu.VMEM)
    smem = pl.BlockSpec(memory_space=pltpu.SMEM)
    patch_grad, text_grad, stats = pl.pallas_call(
        kernel,
        out_shape=(
            jax.ShapeDtypeStruct((ROWS, D), BF16),
            jax.ShapeDtypeStruct((1, D), BF16),
            jax.ShapeDtypeStruct((3,), F32),
        ),
        in_specs=[spec] * 6 + [smem] * 2,
        out_specs=(spec, spec, smem),
        scratch_shapes=scratch,
        compiler_params=pltpu.CompilerParams(
            collective_id=0, has_side_effects=True, vmem_limit_bytes=56 * 2**20
        ),
    )(
        patches.reshape(ROWS, D), weight_in, weight_out.T,
        jnp.concatenate([norm_gain, norm_bias, bias_out, bias_in]).reshape(1, 3 * D + FF),
        text_embed, pair_label.reshape(1, 256), logit_params, counts.reshape(1),
    )
    return patch_grad.reshape(patches.shape), text_grad, stats


def solution(mesh):
    return jax.shard_map(
        shards,
        mesh=mesh,
        in_specs=(
            P("dp", "blk", None, None),
            P("dp", "blk", None),
            P(),
            P(),
            P("dp", None),
            P(),
            P(None, "dp"),
            P(),
            P(("dp", "blk"), None),
            P(),
            P(),
        ),
        out_specs=(P("dp", "blk", None, None), P(("dp", "blk"), None), P()),
        check_vma=False,
    )
```

```python
import jax
import jax.numpy as jnp
from jax import lax
from jax.experimental import pallas as pl
from jax.experimental.pallas import tpu as pltpu
from jax.sharding import PartitionSpec as P

D = 1152
FF = 4304
ROWS = 256
NORM_EPS = 1e-06
GELU_SCALE = 0.7978845608028654
GELU_CUBIC = 0.044715
MESH = pl.DeviceIdType.MESH
F32 = jnp.float32
BF16 = jnp.bfloat16
NT_IN = 34
N_COPIES = 240


def dev(x, y, z, c):
    x, y, z, c = x % 4, y % 4, z % 8, c % 2
    return ((y // 2) * 16 + z * 2 + c, x * 2 + y % 2)


def nt_dot(a, b):
    return lax.dot_general(a, b, (((1,), (1,)), ((), ())), preferred_element_type=F32)


def nn_dot(a, b):
    return jnp.dot(a, b, preferred_element_type=F32)


def split3(v):
    hi = v.astype(BF16)
    rest = v - hi.astype(F32)
    mid = rest.astype(BF16)
    low = (rest - mid.astype(F32)).astype(BF16)
    return hi, mid, low


def exact_dot(v, w, dot):
    rows = v.shape[0]
    hi, mid, low = split3(v)
    res = dot(jnp.concatenate([hi, mid, low], axis=0), w)
    return res[:rows] + res[rows : 2 * rows] + res[2 * rows :]


def rows8(v):
    return jnp.broadcast_to(v, (8, v.shape[1]))


def kernel(
    x_ref, wi_in, wo_in, vec_in, text_in, lab_in, lp_ref, cnt_ref,
    out_ref, tg_ref, st_ref,
    G, W, PM, XP, PLAIN, RSTD, NM, SL, HS, AF, ACC, RW, RO, SF, VP,
    TROW, TCOL, TB, HA, PB, PR, GB, AB, AR, ICOL, DB, DT,
    WS, BS, VEC,
    SS, RS,
):
    dp, blk = lax.axis_index("dp"), lax.axis_index("blk")
    yh, z, c = dp // 16, (dp // 2) % 8, dp % 2
    x, yl = blk // 2, blk % 2
    y = yh * 2 + yl
    cross = dev(x, y + 3 + 2 * yl, z, c)
    share = dev(x, yh * 2 + 1 - yl, z, c)
    partner = dev(x, y, z, c + 1)
    zp, zm = dev(x, y, z + 1, c), dev(x, y, z + 7, c)
    xp, xm = dev(x + 1, y, z, c), dev(x + 3, y, z, c)
    u, v, s = z * 2 + c, x * 4 + y, x * 2 + c
    col_peers = [((u + d) % 16) for d in range(1, 16)]
    col_devs = [dev(x, y, p // 2, p % 2) for p in col_peers]
    plane_peers = [((v + d) % 16) for d in range(1, 16)]
    plane_devs = [dev(p // 4, p % 4, z, c) for p in plane_peers]
    ring_peers = [((s + d) % 8) for d in range(1, 8)]
    ring_devs = [dev(p // 2, y, z, p % 2) for p in ring_peers]

    bar = pltpu.get_barrier_semaphore()
    greet = col_devs + plane_devs + [dev(x + d, y, z, c + 1) for d in (1, 2, 3)]
    greet += [dev(x, y + 3 + 2 * yl, z + d, c) for d in (1, 2, 6, 7)]
    for peer in greet:
        pl.semaphore_signal(bar, inc=1, device_id=peer, device_id_type=MESH)

    copies = {}

    def send(name, src, dst, device):
        k = len(copies)
        cp = pltpu.make_async_remote_copy(
            src_ref=src, dst_ref=dst, send_sem=SS.at[k], recv_sem=RS.at[k], device_id=device, device_id_type=MESH
        )
        cp.start()
        copies[name] = cp

    def same(name, ref, device):
        send(name, ref, ref, device)

    def got(name):
        copies[name].wait_recv()

    def fold(rows, first, count):
        parts = []
        for a in range(0, 8, 2):
            blocks = []
            for b in range(2):
                if a + b < count:
                    t = first + a + b
                    piece = rows[:, 128 * t : 128 * t + 128]
                    blocks.append(pltpu.roll(piece, 4, 0) if b else piece)
            parts.append(sum(blocks) if blocks else jnp.zeros((8, 128), F32))
        return jnp.concatenate(parts, axis=0).astype(BF16)

    for k, w_ref in ((0, wi_in), (1, wo_in)):
        WS[k, :, 4224:4352] = jnp.zeros((48, 128), BF16)
        WS[k, 32:48, :] = jnp.zeros((16, 4352), BF16)
        WS[k, 0:32, 0:FF] = w_ref[0:32, :]
        WS[k, 32:36, 0:FF] = w_ref[32:36, :]
    wi_ref, wo_ref = WS.at[0], WS.at[1]
    BS[:, 4224:4352] = jnp.zeros((1, 128), F32)
    BS[:, 0:FF] = vec_in[:, 3 * D :]
    VEC[...] = jnp.zeros((8, D), F32)
    VEC[0:1, :] = vec_in[:, 0 * D : 1 * D]
    VEC[1:2, :] = vec_in[:, 1 * D : 2 * D]
    VEC[2:3, :] = vec_in[:, 2 * D : 3 * D]
    VEC[3:4, :] = text_in[...].astype(F32)
    wi_tail = wi_ref[32:48, :].astype(F32)[0:8]
    for q in range(4):
        for t in range(8):
            G[yh, 0, c, q, 5 * (t // 4) + t % 4] = wi_ref[0:32, 1024 * q + 128 * t : 1024 * q + 128 * t + 128]
        G[yh, 0, c, q, 4] = fold(wi_tail, 8 * q, 8)
    wo_first = 8 * x + x // 2
    wo_cols = pl.ds(pl.multiple_of(128 * wo_first, 128), 1152)
    wo_main = wo_ref[0:32, wo_cols]
    wo_tail = wo_ref[32:48, wo_cols].astype(F32)[0:8]
    for t in range(2):
        W[yh, 0, c, t] = wi_ref[0:32, 4096 + 128 * t : 4096 + 128 * t + 128]
    for t in range(9):
        W[yh, 0, c, 3 + t] = wo_main[:, 128 * t : 128 * t + 128]
    tail = jnp.concatenate([wi_tail[:, 4096:4352], wo_tail], axis=1)
    W[yh, 0, c, 2] = fold(tail, 0, 8)
    W[yh, 0, c, 12] = fold(tail, 8, 3)

    pl.semaphore_wait(bar, len(greet))

    other = 1 - yh
    both = slice(None)
    mine5 = pl.ds(4 * yl, 5)
    mine4 = pl.ds(5 * yl, 4)
    slots = [0, pl.ds(1, 2), pl.ds(3, 2), pl.ds(5, 2), 7]

    zpp, zmm = dev(x, y, z + 2, c), dev(x, y, z + 6, c)
    other5 = pl.ds(4 * (1 - yl), 5)

    def z_own(k, device, over):
        send(("zA", k), G.at[yh, 0, c, x, mine5], G.at[yh, k, c, x, mine5], device)
        send(("zB", k), G.at[yh, 0, c, x, other5], G.at[yh, k, c, x, other5], over)

    def z_forward():
        for a in (0, 1):
            send(("zF", 5, a), G.at[a, 3, c, x, mine5], G.at[a, 5, c, x, mine5], zp)
            send(("zF", 6, a), G.at[a, 4, c, x, mine5], G.at[a, 6, c, x, mine5], zm)
        send(("zF", 7), G.at[0, 3, c, x, mine5], G.at[0, 7, c, x, mine5], zpp)
        send(("zF", 8), G.at[1, 4, c, x, mine5], G.at[1, 7, c, x, mine5], zmm)

    chain_r, chain_l = (0, 1, 3, 5, 7), (0, 2, 4, 6, 7)

    part_in, part_out = pl.ds(0, 3), pl.ds(3, 10)

    def w_send(name, sel, src, dst, tiles, device):
        send(name, W.at[sel, src, c, tiles], W.at[sel, dst, c, tiles], device)

    def di_send(n):
        w_send(("iR", n), both if n < 3 else 0, chain_r[n], chain_r[n + 1], part_in, zp)
        w_send(("iL", n), both if n < 3 else 1, chain_l[n], chain_l[n + 1], part_in, zm)

    def di_in(n):
        got(("iR", n - 1))
        got(("iL", n - 1))
        if n < 4:
            di_send(n)

    def d_send(n, a, sel):
        if n < 3 or a == 0:
            w_send(("dR", n, a), sel, chain_r[n], chain_r[n + 1], part_out, zp)
        if n < 3 or a == 1:
            w_send(("dL", n, a), sel, chain_l[n], chain_l[n + 1], part_out, zm)

    def d_in(n, a):
        if n < 4 or a == 0:
            got(("dR", n - 1, a))
        if n < 4 or a == 1:
            got(("dL", n - 1, a))
        if n < 4:
            d_send(n, a, yh if a == 0 else other)

    def d_partner(n):
        same(("pD", n), W.at[:, slots[n], c, part_out], partner)

    def y_send(name, sel, g, q, device):
        same((name, g), G.at[sel, slots[g], c, q % 4, mine4], device)

    def x_send(g):
        sel = other if g == 0 else both
        same(("xR", g), G.at[sel, slots[g], c, x, mine5], xp)
        same(("xL", g), G.at[sel, slots[g], c, x, mine5], xm)
        if g != 0:
            y_send("yA", both, g, x, cross)

    def x_in(g):
        got(("xR", g))
        got(("xL", g))
        sel = other if g == 0 else both
        same(("fR", g), G.at[other if g == 0 else 0, slots[g], c, (x + 3) % 4, mine5], xp)
        if g != 0:
            same(("fL", g), G.at[1, slots[g], c, (x + 1) % 4, mine5], xm)
        y_send("yB", sel, g, x + 3, share)
        y_send("yC", sel, g, x + 1, share)

    def f_in(g):
        got(("fR", g))
        if g != 0:
            got(("fL", g))
            y_send("yD", both, g, x + 2, cross)
        same(("pF", g), G.at[:, slots[g], c, :, mine5], partner)

    def y_in(g):
        for name in ("yA", "yB", "yC", "yD"):
            got((name, g))
        same(("pG", g), G.at[:, slots[g], c, :, pl.ds(5 * (1 - yl), 4)], partner)

    yc = y + 3 + 2 * yl
    z_own(1, zp, dev(x, yc, z + 1, c))
    z_own(2, zm, dev(x, yc, z + 7, c))
    same(("e1",), G.at[yh, 0, c, x, other5], cross)
    text_f = VEC[3:4, :]
    txt_norm = jnp.sqrt(jnp.sum(text_f * text_f, axis=1, keepdims=True) + NORM_EPS)
    txt_unit = text_f / txt_norm
    TROW[...] = txt_unit
    TCOL[u] = jnp.concatenate([txt_unit.astype(BF16).astype(F32), jnp.zeros((1, 128), F32)], axis=1)

    for i, device in enumerate(col_devs):
        same(("t1", i), TCOL.at[u], device)
    z_own(3, zpp, dev(x, yc, z + 2, c))
    z_own(4, zmm, dev(x, yc, z + 6, c))
    same(("i1",), W.at[yh, 0, c, part_in], cross)
    y_send("yA", yh, 0, x, cross)
    y_send("yD", yh, 0, x + 2, cross)
    lane = lax.broadcasted_iota(jnp.int32, (1, D), 1)
    rest = lane - 1024
    place = jnp.where(lane < 1024, lane >> 5, rest >> 2)
    row_in = jnp.where(lane < 1024, lane & 31, 32 + (rest & 3))
    slot = (place >> 1) & 7
    steps = ((slot + 1) >> 1) * (1 - 2 * (slot & 1))
    shard = (place >> 4) * 16 + ((z + 8 + steps) & 7) * 2 + (place & 1)
    natural = 36 * shard + row_in

    @pl.loop(0, 9)
    def _(i):
        first = pl.multiple_of(128 * i, 128)
        rows = lax.broadcasted_iota(jnp.int32, (128, D), 0) + 128 * i
        PM[pl.ds(first, 128), :] = jnp.where(rows == natural, 1.0, 0.0).astype(BF16)

    got(("e1",))
    x_send(0)
    got(("i1",))
    VP[...] = exact_dot(VEC[...], PM[...], nn_dot)
    gain, nbias, bout = VP[0:1, :], VP[1:2, :], VP[2:3, :]
    count = jnp.zeros((1, 128), F32)[:, 0:1] + cnt_ref[0].astype(F32)

    for k in (1, 2):
        got(("zA", k))
        got(("zB", k))
    x_send(1)
    for k in (3, 4):
        got(("zA", k))
        got(("zB", k))
    z_forward()
    x_send(2)
    di_send(0)
    same(("d1",), W.at[yh, 0, c, part_out], cross)
    d_send(0, 0, yh)
    x_in(0)
    @pl.loop(0, 4)
    def _(i):
        rows = pl.ds(pl.multiple_of(64 * i, 64), 64)
        xs = nn_dot(x_ref[rows, :], PM[...])
        XP[rows, :] = xs
        centre = xs - jnp.mean(xs, axis=1, keepdims=True)
        inv = lax.rsqrt(jnp.mean(centre * centre, axis=1, keepdims=True) + NORM_EPS)
        plain = centre * inv
        PLAIN[rows, :] = plain
        RSTD[rows, :] = jnp.broadcast_to(inv, (64, 128))
        NM[rows, :] = (plain * gain + nbias).astype(BF16)

    x_in(1)
    for k in (5, 6):
        for a in (0, 1):
            got(("zF", k, a))
    x_send(3)
    for k in (7, 8):
        got(("zF", k))
    x_send(4)
    di_in(1)
    row_ids = lax.broadcasted_iota(jnp.int32, (ROWS, 1), 0).astype(F32)
    valid = row_ids < count
    xsum = jnp.sum(jnp.where(valid, XP[...], 0.0), axis=0, keepdims=True)

    got(("d1",))
    d_send(0, 1, other)
    x_in(2)
    f_in(0)
    f_in(1)
    d_in(1, 0)
    di_in(2)
    y_in(0)
    @pl.loop(0, 8)
    def _(i):
        r = lax.broadcasted_iota(jnp.int32, (128, 1024), 0)
        col = lax.broadcasted_iota(jnp.int32, (128, 1024), 1)
        SF[pl.ds(pl.multiple_of(128 * i, 128), 128), :] = jnp.where(
            col == 32 * (r >> 2) + 4 * i + (r & 3), 1.0, 0.0
        ).astype(BF16)

    x_in(3)
    f_in(2)
    x_in(4)
    d_in(1, 1)
    di_in(3)
    y_in(1)
    labels_nat = jnp.broadcast_to(lab_in[...].astype(F32), (16, 256))

    def natural_pair(v_, u_):
        return ((((v_ >> 1) & 1) * 16 + u_) * 8) + ((v_ >> 2) * 2) + (v_ & 1)

    row256 = lax.broadcasted_iota(jnp.int32, (256, 256), 0)
    col256 = lax.broadcasted_iota(jnp.int32, (256, 256), 1)
    labels_b = labels_nat.astype(BF16)
    labels = nn_dot(labels_b, jnp.where(row256 == natural_pair(col256 >> 4, col256 & 15), 1.0, 0.0).astype(BF16))[0:1]
    own_label = jnp.sum(jnp.where(col256[0:1] == v * 16 + u, labels, 0.0), axis=1, keepdims=True)
    lab_img = nn_dot(
        labels_b, jnp.where(row256[:, :128] == natural_pair(v, col256[:, :128] & 15), 1.0, 0.0).astype(BF16)
    )[0:1, :16]
    lab_txt = jnp.sum(
        jnp.where(col256[:16] == natural_pair(row256[:16], u), labels_nat, 0.0), axis=1, keepdims=True
    )

    f_in(3)
    d_in(2, 0)
    f_in(4)
    y_in(2)
    di_in(4)
    same(("pI",), W.at[:, :, c, part_in], partner)
    d_in(2, 1)
    for i in range(15):
        got(("t1", i))
    block = TCOL[...].reshape(16, 1280).astype(BF16)
    TB[c, v] = jnp.where(c == 0, block[:, :640].astype(F32), block[:, 640:].astype(F32)).astype(BF16)
    def unfold(store, pieces):
        res = nn_dot(SF[...], jnp.concatenate([p.reshape(1024, 128) for p in pieces], axis=1)).astype(BF16)
        for j in range(len(pieces)):
            for a in range(8):
                store(j, a, res[128 * a : 128 * a + 128, 128 * j : 128 * j + 128])

    def store_in(base):
        def store(j, a, tile):
            RW[8 * (base + j) + a] = tile
        return store

    def store_direct(j, a, tile, first=0):
        t = first + a
        if t < 2:
            RW[32 + t] = tile
        elif t < 11:
            RO[t - 2] = tile

    def fwd(first, count_tiles, main_tiles):
        wm = jnp.concatenate([m.reshape(1024, 128) for m in main_tiles], axis=1)
        wr = jnp.concatenate([RW[first + t] for t in range(count_tiles)], axis=1)
        pre_all = nn_dot(NM[:, :1024], wm) + nn_dot(NM[:, 1024:], wr)
        bias = BS[:, pl.ds(pl.multiple_of(128 * first, 128), 128 * count_tiles)]
        for t in range(count_tiles):
            pre = pre_all[:, 128 * t : 128 * t + 128] + bias[:, 128 * t : 128 * t + 128]
            sq = pre * pre
            th = jnp.tanh(GELU_SCALE * pre * (1.0 + GELU_CUBIC * sq))
            half = 0.5 * (1.0 + th)
            hid = pre * half
            SL[first + t] = half + 0.5 * pre * (1.0 - th * th) * (GELU_SCALE + 3.0 * GELU_SCALE * GELU_CUBIC * sq)
            HS[first + t] = jnp.sum(jnp.where(valid, hid, 0.0), axis=0, keepdims=True)

    def fwd_pair(start):
        @pl.loop(start, start + 2)
        def _(p):
            q, half = p // 2, p % 2
            fwd(4 * p, 4, [G[:, :, :, q, 5 * half + t] for t in range(4)])

    y_in(3)
    for g in range(5):
        got(("pF", g))
    got(("pI",))
    for q in (0, 2):
        unfold(store_in(q), [G[:, :, :, q, 4], G[:, :, :, q + 1, 4]])
    unfold(store_direct, [W[:, :, :, 2]])

    y_in(4)
    for g in range(3):
        d_partner(g)
    for i, device in enumerate(plane_devs):
        same(("t2", i), TB.at[c, v], device)
    fwd(32, 2, [W[:, :, :, 0], W[:, :, :, 1]])
    for g in range(5):
        got(("pG", g))

    fwd_pair(0)
    d_in(3, 0)
    d_in(3, 1)
    fwd_pair(2)
    d_partner(3)
    fwd_pair(4)
    fwd_pair(6)
    d_in(4, 0)
    d_in(4, 1)
    d_partner(4)

    def first_tile(member):
        return 4 * member + member // 4

    for i, (p, device) in enumerate(zip(ring_peers, ring_devs)):
        send(("h", i), HS.at[pl.ds(first_tile(p), 5)], HA.at[s], device)
    HA[s] = HS[pl.ds(first_tile(s), 5)]
    for i in range(15):
        got(("t2", i))
    same(("t3",), TB.at[c], partner)
    for g in range(5):
        got(("pD", g))
    unfold(lambda j, a, tile: store_direct(j, a, tile, 8), [W[:, :, :, 12]])
    for i in range(7):
        got(("h", i))
    last_mine = jnp.where(s % 4 == 3, 1.0, 0.0)
    part_m = jnp.zeros((24, 1024), F32)
    part_r = jnp.zeros((24, 128), F32)
    for t in range(5):
        col = HA[:, t].reshape(8, 128)
        if t == 4:
            col = col * last_mine
        lhs = jnp.concatenate(split3(col), axis=0)
        part_m += nt_dot(lhs, W[:, :, :, 3 + 4 * c + t].reshape(1024, 128))
        part_r += nt_dot(lhs, RO[4 * c + t])
    part = jnp.concatenate([part_m, part_r], axis=1)
    part = part[0:8] + part[8:16] + part[16:24]
    for j in range(8):
        PB[j] = part[j : j + 1]
    for i, (p, device) in enumerate(zip(ring_peers, ring_devs)):
        send(("p", i), PB.at[p], PR.at[s], device)
    PR[s] = PB[s]
    got(("t3",))
    texts_nat = jnp.concatenate([TB[0].reshape(256, 640), TB[1].reshape(256, 640)[:, :512]], axis=1)
    texts = nn_dot(texts_nat, PM[...]).astype(BF16)
    for i in range(7):
        got(("p", i))
    mixed = jnp.sum(PR[...].reshape(8, D), axis=0, keepdims=True)
    pooled = (xsum + mixed) / count + bout

    img_norm = jnp.sqrt(jnp.sum(pooled * pooled, axis=1, keepdims=True) + NORM_EPS)
    img_unit = pooled / img_norm
    img_b = img_unit.astype(BF16)
    scale = jnp.exp(jnp.zeros((1, 128), F32) + lp_ref[0])[:, 0:1]
    shift = lp_ref[1]
    def terms(inner, same_label):
        logits = scale * inner + shift
        sign = jnp.where(same_label, 1.0, -1.0)
        neg = -sign * logits
        soft = jnp.maximum(neg, 0.0) + jnp.log1p(jnp.exp(-jnp.abs(neg)))
        return soft, -sign / (1.0 + jnp.exp(-neg))

    img_rows = jnp.broadcast_to(img_b.astype(F32), (16, D)).astype(BF16)
    inner = nt_dot(img_rows, texts)[0:8]
    soft, grad = terms(inner, labels == own_label)
    d_img = scale * exact_dot(grad, texts, nn_dot)[0:1]
    d_pooled = (d_img - img_unit * jnp.sum(img_unit * d_img, axis=1, keepdims=True)) / img_norm
    row_grad = d_pooled / count

    GB[s] = row_grad
    for i, device in enumerate(ring_devs):
        same(("g", i), GB.at[s], device)
    stats = [
        jnp.sum(soft[0:1], axis=1, keepdims=True),
        jnp.sum((grad * scale * inner)[0:1], axis=1, keepdims=True),
        jnp.sum(grad[0:1], axis=1, keepdims=True),
    ]
    lane128 = lax.broadcasted_iota(jnp.int32, (1, 128), 1)
    stat_row = sum(jnp.where(lane128 == k, stats[k], 0.0) for k in range(3))
    img_nat = nt_dot(img_rows, PM[...])[0:1]
    ICOL[u] = jnp.concatenate([img_nat, stat_row], axis=1)
    for i, device in enumerate(col_devs):
        same(("i1", i), ICOL.at[u], device)
    for i in range(7):
        got(("g", i))
    grads = GB[...].reshape(8, D).astype(BF16)
    for t in range(5):
        res = nn_dot(grads[:, :1024], W[:, :, :, 3 + 4 * c + t].reshape(1024, 128)) + nn_dot(
            grads[:, 1024:], RO[4 * c + t]
        )
        for j in range(8):
            AB[j, t] = res[j : j + 1]
    for i, (p, device) in enumerate(zip(ring_peers, ring_devs)):
        send(("a", i), AB.at[p], AR.at[s], device)
    AR[s] = AB[s]

    for i in range(15):
        got(("i1", i))
    column = ICOL[...].reshape(16, 1280)
    imgs = column[:, :D].astype(BF16)
    pick = (
        lax.broadcasted_iota(jnp.int32, (16, 256), 1) == 16 * lax.broadcasted_iota(jnp.int32, (16, 256), 0) + u
    )
    texts16 = nn_dot(jnp.where(pick, 1.0, 0.0).astype(BF16), texts_nat).astype(BF16)
    _, grad_t = terms(nt_dot(texts16, imgs), lab_txt == lab_img)
    d_part = exact_dot(grad_t, imgs, nn_dot)
    col_stats = jnp.sum(column[:, D:], axis=0, keepdims=True)
    for k in range(16):
        DB[k] = jnp.concatenate([d_part[k : k + 1], col_stats], axis=1)
    for i, (p, device) in enumerate(zip(plane_peers, plane_devs)):
        send(("i2", i), DB.at[p], DT.at[v], device)
    DT[v] = DB[v]

    for i in range(7):
        got(("a", i))

    def act_tile(t):
        member = 0
        while member < 7 and first_tile(member + 1) <= t:
            member += 1
        return AR[member, t - first_tile(member)]

    for t in range(NT_IN):
        AF[t] = act_tile(t)

    def bwd(first, count_tiles, main_tiles, start):
        pg = jnp.concatenate([(AF[first + t] * SL[first + t]).astype(BF16) for t in range(count_tiles)], axis=1)
        wm = jnp.concatenate([m.reshape(1024, 128) for m in main_tiles], axis=1)
        wr = jnp.concatenate([RW[first + t] for t in range(count_tiles)], axis=1)
        if start:
            ACC[:, :1024] = nt_dot(pg, wm)
            ACC[:, 1024:] = nt_dot(pg, wr)
        else:
            ACC[:, :1024] += nt_dot(pg, wm)
            ACC[:, 1024:] += nt_dot(pg, wr)

    bwd(32, 2, [W[:, :, :, 0], W[:, :, :, 1]], True)

    @pl.loop(0, 8)
    def _(p):
        q, half = p // 2, p % 2
        bwd(4 * p, 4, [G[:, :, :, q, 5 * half + t] for t in range(4)], False)

    @pl.loop(0, 4)
    def _(i):
        rows = pl.ds(pl.multiple_of(64 * i, 64), 64)
        plain = PLAIN[rows, :]
        q = ACC[rows, :] * VP[0:1, :]
        mean_q = jnp.mean(q, axis=1, keepdims=True)
        mean_qp = jnp.mean(q * plain, axis=1, keepdims=True)
        total = row_grad + RSTD[rows, 0:1] * (q - mean_q - plain * mean_qp)
        ids = (lax.broadcasted_iota(jnp.int32, (64, 1), 0) + 64 * i).astype(F32)
        scaled = jnp.where(ids < count, 256.0 * total, 0.0).astype(BF16)
        out_ref[rows, :] = nt_dot(scaled, PM[...]).astype(BF16)

    for i in range(15):
        got(("i2", i))
    sums = jnp.sum(DT[...].reshape(16, 1280), axis=0, keepdims=True)
    for k in range(3):
        st_ref[k] = jnp.sum(jnp.where(lane128 == k, sums[:, D:], 0.0)) / 256.0
    d_txt = scale * sums[:, :D]
    unit = TROW[...]
    tg = (d_txt - unit * jnp.sum(unit * d_txt, axis=1, keepdims=True)) / jnp.sqrt(
        jnp.sum(VEC[3:4, :] * VEC[3:4, :], axis=1, keepdims=True) + NORM_EPS
    )
    tg_ref[...] = tg.astype(BF16)

    for cp in copies.values():
        cp.wait_send()


def shards(
    patches, counts, norm_gain, norm_bias, weight_in, bias_in, weight_out, bias_out, text_embed, pair_label,
    logit_params,
):
    vm = pltpu.VMEM
    scratch = [
        vm((2, 8, 2, 4, 9, 32, 128), BF16),
        vm((2, 8, 2, 13, 32, 128), BF16),
        vm((D, D), BF16),
        vm((ROWS, D), F32),
        vm((ROWS, D), F32),
        vm((ROWS, 128), F32),
        vm((ROWS, D), BF16),
        vm((NT_IN, ROWS, 128), F32),
        vm((NT_IN, 1, 128), F32),
        vm((NT_IN, 1, 128), F32),
        vm((ROWS, D), F32),
        vm((NT_IN, 128, 128), BF16),
        vm((9, 128, 128), BF16),
        vm((1024, 1024), BF16),
        vm((8, D), F32),
        vm((1, D), F32),
        vm((16, 1, 1280), F32),
        vm((2, 16, 16, 640), BF16),
        vm((8, 5, 1, 128), F32),
        vm((8, 1, D), F32),
        vm((8, 1, D), F32),
        vm((8, 1, D), F32),
        vm((8, 5, 1, 128), F32),
        vm((8, 5, 1, 128), F32),
        vm((16, 1, 1280), F32),
        vm((16, 1, 1280), F32),
        vm((16, 1, 1280), F32),
        vm((2, 48, 4352), BF16),
        vm((1, 4352), F32),
        vm((8, D), F32),
        pltpu.SemaphoreType.DMA((N_COPIES,)),
        pltpu.SemaphoreType.DMA((N_COPIES,)),
    ]
    spec = pl.BlockSpec(memory_space=pltpu.VMEM)
    smem = pl.BlockSpec(memory_space=pltpu.SMEM)
    patch_grad, text_grad, stats = pl.pallas_call(
        kernel,
        out_shape=(
            jax.ShapeDtypeStruct((ROWS, D), BF16),
            jax.ShapeDtypeStruct((1, D), BF16),
            jax.ShapeDtypeStruct((3,), F32),
        ),
        in_specs=[spec] * 6 + [smem] * 2,
        out_specs=(spec, spec, smem),
        scratch_shapes=scratch,
        compiler_params=pltpu.CompilerParams(
            collective_id=0, has_side_effects=True, vmem_limit_bytes=56 * 2**20
        ),
    )(
        patches.reshape(ROWS, D), weight_in, weight_out.T,
        jnp.concatenate([norm_gain, norm_bias, bias_out, bias_in]).reshape(1, 3 * D + FF),
        text_embed, pair_label.reshape(1, 256), logit_params, counts.reshape(1),
    )
    return patch_grad.reshape(patches.shape), text_grad, stats


def solution(mesh):
    return jax.shard_map(
        shards,
        mesh=mesh,
        in_specs=(
            P("dp", "blk", None, None),
            P("dp", "blk", None),
            P(),
            P(),
            P("dp", None),
            P(),
            P(None, "dp"),
            P(),
            P(("dp", "blk"), None),
            P(),
            P(),
        ),
        out_specs=(P("dp", "blk", None, None), P(("dp", "blk"), None), P()),
        check_vma=False,
    )
```
